256 devices in a mesh: region: 8 (over y, z_lo), slab: 32 (over z_hi, x, core).
Axes of the slice: x: 4, y: 4, z: 8 (z_hi: 4, z_lo: 2; z = z_hi * 2 + z_lo), core: 2. Of those that a mesh axis runs over, the one named last changes fastest.
Arguments:
- magnetic: float32 [3, 512, 64, 1024], P(None, 'slab', None, 'region'), may hold values from -6 to 6
- velocity: float32 [3, 512, 64, 1024], P(None, 'slab', None, 'region'), may hold values from -12 to 12
- wall_response: float32 [1024, 512, 512], P(('region', 'slab')), may hold values from -0.25 to 0.25
- mode_slots: int32 [1024], replicated, may hold values from 0 to 1023, each once
- wall_layers: int32 [1024], P('region'), may hold values from 1 to 8
Outputs:
- magnetic_next: float32 [3, 512, 64, 1024], P(None, 'slab', None, 'region')
- wall_flux: float32 [2, 512, 1024], P(None, 'slab', 'region')
The draws below stay inside these ranges and needn't reach their ends.
Inputs may be any that keep to these rules, and one draw needn't show every extreme that they name: `mode_slots`: each slot names a different mode.
All inputs are finite; a program needn't handle non-finite values.
Results may differ from the reference program's by a relative error of at most 0.00007.
Values sent between devices are 32-bit elements; how exact they have to be, the bound alone decides.
No kernel may reach another device: no remote copies, remote signals or barrier semaphores. Data moves between devices by JAX's collectives and lax.ppermute only.
A program may use at most 128 MiB of HBM per device.

```python
import math
import jax
import jax.numpy as jnp
from jax import lax

NR = 64
LW = 8
NZ = 512
NPHI = 1024


def set_ends(array, rng, low, top_value):
    shape = array.shape
    index_at = [jax.random.randint(jax.random.fold_in(rng, axis), (), 0, shape[axis]) for axis in range(len(shape))]
    array = array.at[tuple(index_at)].set(low)
    longest = shape.index(max(shape))
    index_at[longest] = (index_at[longest] + 1) % shape[longest]
    return array.at[tuple(index_at)].set(top_value)


def levels(key, dims, pieces, least, top_value):
    factor_of, own = 1.0, jax.random.fold_in(key, 6)
    for position, parts in pieces:
        heights = jnp.exp(jax.random.uniform(jax.random.fold_in(own, position), (parts,), jnp.float32, least / len(pieces), top_value / len(pieces)))
        factor_of = factor_of * jnp.repeat(heights, dims[position] // parts).reshape([-1 if axis == position else 1 for axis in range(len(dims))])
    return factor_of


def scatter_about(key, extent, width, limit, shards=(), held_as=jnp.bfloat16):
    values = jax.random.normal(key, extent, jnp.float32) * width
    if len(shards) > 0:
        values = levels(key, extent, shards, -0.22, 0.18) * values
    return jnp.clip(values, min=-limit, max=limit).astype(held_as)


def setup_inputs(seed: int = 0) -> dict:
    splits = jax.random.split(jax.random.key(seed), 6)
    magnetic = scatter_about(splits[0], (3, NZ, NR, NPHI), 1.0, 6.0, ((1, 32), (3, 8)), jnp.float32)
    velocity = scatter_about(splits[1], (3, NZ, NR, NPHI), 2.0, 12.0, ((1, 32), (3, 8)), jnp.float32)
    wall_response = scatter_about(splits[2], (NPHI, NZ, NZ), NZ ** -0.5, 0.25, ((0, 256),), jnp.float32)
    mode_slots = jax.random.permutation(splits[3], NPHI).astype(jnp.int32)
    wall_layers = set_ends(jax.random.randint(splits[4], (NPHI,), 1, LW + 1), jax.random.fold_in(splits[4], 1), 1, LW).astype(jnp.int32)
    return {"magnetic": magnetic, "velocity": velocity, "wall_response": wall_response, "mode_slots": mode_slots, "wall_layers": wall_layers}


TIME_STEP = 3.0e-4
DIFFUSIVITY = 1.0e-3
RADIAL_STEP = 1.0 / 384.0
AXIAL_STEP = 1.0 / 768.0
HIGHEST = lax.Precision.HIGHEST


def basis_table(modes, cells, azimuth_total):
    frequency = (modes + 1) // 2
    phase = (frequency[:, None] * (2 * cells[None, :] + 1)) % (2 * azimuth_total)
    angle = phase.astype(jnp.float32) * (math.pi / azimuth_total)
    return jnp.where((modes % 2 == 1)[:, None], jnp.sin(angle), jnp.cos(angle))


def mode_weight(modes, azimuth_total):
    single = (modes == 0) | (modes == azimuth_total - 1)
    return jnp.where(single, 1.0, 2.0).astype(jnp.float32) / azimuth_total


def radius_column(radial_cells):
    index = jnp.arange(radial_cells).astype(jnp.float32)
    return (1.0 - (radial_cells - index - 0.5) * RADIAL_STEP)[:, None]


def advance(center_b, center_u, radial_b, radial_u, azimuth_b, azimuth_u, axial_b, axial_u, radius, angle_step):
    inv_radial = 1.0 / (2.0 * RADIAL_STEP)
    inv_azimuth = 1.0 / (2.0 * radius * angle_step)
    inv_axial = 1.0 / (2.0 * AXIAL_STEP)
    grad_b = ((radial_b[0] - radial_b[1]) * inv_radial, (azimuth_b[0] - azimuth_b[1]) * inv_azimuth, (axial_b[0] - axial_b[1]) * inv_axial)
    grad_u = ((radial_u[0] - radial_u[1]) * inv_radial, (azimuth_u[0] - azimuth_u[1]) * inv_azimuth, (axial_u[0] - axial_u[1]) * inv_axial)
    laplace = (radial_b[0] - 2.0 * center_b + radial_b[1]) / RADIAL_STEP ** 2
    laplace = laplace + grad_b[0] / radius
    laplace = laplace + (azimuth_b[0] - 2.0 * center_b + azimuth_b[1]) / (radius * angle_step) ** 2
    laplace = laplace + (axial_b[0] - 2.0 * center_b + axial_b[1]) / AXIAL_STEP ** 2
    carried = center_u[0] * grad_b[0] + center_u[1] * grad_b[1] + center_u[2] * grad_b[2]
    stretched = center_b[0] * grad_u[0] + center_b[1] * grad_u[1] + center_b[2] * grad_u[2]
    return center_b + TIME_STEP * (DIFFUSIVITY * laplace - carried + stretched)


def pad_around(values):
    padded = jnp.pad(values, ((0, 0), (1, 1), (0, 0), (0, 0)))
    return jnp.concatenate([padded[..., -1:], padded, padded[..., :1]], -1)


def neighbours(padded):
    center = padded[:, 1:-1, 1:-1, 1:-1]
    radial = (padded[:, 1:-1, 2:, 1:-1], padded[:, 1:-1, :-2, 1:-1])
    azimuth = (padded[:, 1:-1, 1:-1, 2:], padded[:, 1:-1, 1:-1, :-2])
    axial = (padded[:, 2:, 1:-1, 1:-1], padded[:, :-2, 1:-1, 1:-1])
    return center, radial, azimuth, axial


def reference(magnetic, velocity, wall_response, mode_slots, wall_layers):
    radial_cells = magnetic.shape[2]
    azimuth_total = magnetic.shape[3]
    trace = magnetic[1:3, :, radial_cells - 1, :]
    cells = jnp.arange(azimuth_total, dtype=jnp.int32)
    table = basis_table(mode_slots, cells, azimuth_total)
    coefficients = jnp.einsum("sk,czk->scz", table, trace, precision=HIGHEST)
    responses = jnp.einsum("szy,scy->scz", wall_response, coefficients, precision=HIGHEST)
    weighted = table * mode_weight(mode_slots, azimuth_total)[:, None]
    wall_flux = jnp.einsum("sk,scz->czk", weighted, responses, precision=HIGHEST)
    thickness = wall_layers.astype(jnp.float32) / LW
    ghost = jnp.concatenate([magnetic[0:1, :, radial_cells - 1, :], trace - thickness * wall_flux], 0)
    magnetic_ext = jnp.concatenate([magnetic[:, :, :1], magnetic, ghost[:, :, None]], 2)
    velocity_ext = jnp.concatenate([velocity[:, :, :1], velocity, velocity[:, :, -1:]], 2)
    center_b, radial_b, azimuth_b, axial_b = neighbours(pad_around(magnetic_ext))
    center_u, radial_u, azimuth_u, axial_u = neighbours(pad_around(velocity_ext))
    radius = radius_column(radial_cells)
    angle_step = 2.0 * math.pi / azimuth_total
    magnetic_next = advance(center_b, center_u, radial_b, radial_u, azimuth_b, azimuth_u, axial_b, axial_u, radius, angle_step)
    return magnetic_next, wall_flux
```

```python
import math

import jax
import jax.numpy as jnp
from jax import lax
from jax.experimental import pallas as pl
from jax.experimental.pallas import tpu as pltpu
from jax.sharding import PartitionSpec as P

LW = 8
TIME_STEP = 0.0003
DIFFUSIVITY = 0.001
RADIAL_STEP = 1.0 / 384.0
AXIAL_STEP = 1.0 / 768.0

F32 = jnp.float32
BF16 = jnp.bfloat16
BOTH = ("region", "slab")
VMEM = pl.BlockSpec(memory_space=pltpu.VMEM)
ANY = pl.BlockSpec(memory_space=pl.ANY)
NT = (((1,), (1,)), ((), ()))
NN = (((1,), (0,)), ((), ()))


def params(mib):
    return pltpu.CompilerParams(vmem_limit_bytes=mib * 1024 * 1024)


def cost(flops, nbytes):
    return pl.CostEstimate(flops=flops, bytes_accessed=nbytes, transcendentals=0)


def lanes(shape):
    return lax.broadcasted_iota(jnp.int32, shape, len(shape) - 1)


def rows(shape):
    return lax.broadcasted_iota(jnp.int32, shape, len(shape) - 2)


def split(x):
    high = x.astype(BF16)
    return high, (x - high.astype(F32)).astype(BF16)


def dot(a, b, dims):
    return lax.dot_general(a, b, dims, preferred_element_type=F32)


def dot3(a, b, dims):
    ah, al = a
    bh, bl = b
    return dot(ah, bh, dims) + (dot(ah, bl, dims) + dot(al, bh, dims))


def half_turn_sine(phase, total):
    half = phase - total
    fold = jnp.abs(half)
    fold = jnp.minimum(fold, total - fold)
    x = fold.astype(F32) * (math.pi / total)
    y = x * x
    poly = -1.0 / math.factorial(11)
    for n, sign in ((9, 1.0), (7, -1.0), (5, 1.0), (3, -1.0)):
        poly = poly * y + sign / math.factorial(n)
    value = x + x * (y * poly)
    return jnp.where(half < 0, value, -value)


def block_transpose(x, width):
    r, b = rows(x.shape), lanes(x.shape) // width
    n, m = x.shape
    for bit in range(3):
        h = 1 << bit
        down = pltpu.roll(pltpu.roll(x, h, 0), m - width * h, 1)
        up = pltpu.roll(pltpu.roll(x, n - h, 0), width * h, 1)
        rb, bb = (r >> bit) & 1, (b >> bit) & 1
        x = jnp.where(rb == bb, x, jnp.where(rb == 1, down, up))
    return x


def encode_kernel(mag, modes, message, table, edge, coeff, sem):
    nmodes, cells = table.shape
    copy = pltpu.make_async_copy(mag.at[1:3, :, 56:64, :], edge, sem)
    copy.start()
    first = lax.axis_index("region") * cells
    odd_cell = (2 * (first + lanes((cells, cells))) + 1).astype(F32)
    columns = jnp.transpose(modes[...].astype(F32), (1, 0))
    for j in range(nmodes // cells):
        mode = jnp.broadcast_to(columns[:, j : j + 1], (cells, cells)).astype(jnp.int32)
        phase = (((mode + 1) >> 1).astype(F32) * odd_cell).astype(jnp.int32)
        phase = jnp.where((mode & 1) == 1, phase, phase + nmodes // 2) & (2 * nmodes - 1)
        table[j * cells : (j + 1) * cells, :] = half_turn_sine(phase, nmodes)
    copy.wait()
    trace = edge[:, :, 7, :].reshape(32, cells)
    trace = split(jnp.concatenate([trace] * 4, 0))
    coeff[...] = dot3(split(table[...]), trace, NT)
    count = nmodes // 4
    lane = lanes((count, 128)) // 32
    out = coeff[pl.ds(0, count, stride=4), :]
    for i in range(1, 4):
        out = jnp.where(lane == i, coeff[pl.ds(i, count, stride=4), :], out)
    message[...] = out


def encode(mag, modes):
    cells = mag.shape[3]
    nmodes = modes.size
    return pl.pallas_call(
        encode_kernel,
        out_shape=(
            jax.ShapeDtypeStruct((nmodes // 4, 128), F32),
            jax.ShapeDtypeStruct((nmodes, cells), F32),
        ),
        in_specs=[ANY, VMEM],
        out_specs=(VMEM, VMEM),
        scratch_shapes=[
            pltpu.VMEM((2, 16, 8, cells), F32),
            pltpu.VMEM((nmodes, 128), F32),
            pltpu.SemaphoreType.DMA,
        ],
        compiler_params=params(8),
        cost_estimate=cost(3 * 2 * 1024 * 128 * 128, 1 << 20),
        name="encode",
    )(mag, modes.reshape(8, 128))


def weigh_kernel(table, modes, high, low, scaled):
    nmodes, cells = table.shape
    columns = jnp.transpose(modes[...].astype(F32), (1, 0))
    for j in range(nmodes // cells):
        mode = jnp.broadcast_to(columns[:, j : j + 1], (cells, cells))
        single = (mode == 0.0) | (mode == float(nmodes - 1))
        part = slice(j * cells, (j + 1) * cells)
        scaled[part, :] = table[part, :] * jnp.where(single, 1.0 / nmodes, 2.0 / nmodes)
    for i in range(4):
        high[i], low[i] = split(scaled[pl.ds(i, nmodes // 4, stride=4), :])


def weigh(table, modes):
    nmodes, cells = table.shape
    shape = jax.ShapeDtypeStruct((4, nmodes // 4, cells), BF16)
    return pl.pallas_call(
        weigh_kernel,
        out_shape=(shape, shape),
        in_specs=[VMEM, VMEM],
        out_specs=(VMEM, VMEM),
        scratch_shapes=[pltpu.VMEM((nmodes, cells), F32)],
        compiler_params=params(8),
        cost_estimate=cost(1 << 20, 1 << 20),
        name="weigh",
    )(table, modes.reshape(8, 128))


def halves_kernel(wall, high, low):
    high[...], low[...] = split(wall[...])


def halves(wall):
    shape = jax.ShapeDtypeStruct(wall.shape, BF16)
    block = pl.BlockSpec((1, *wall.shape[1:]), lambda i: (i, 0, 0))
    return pl.pallas_call(
        halves_kernel,
        out_shape=(shape, shape),
        grid=(wall.shape[0],),
        in_specs=[block],
        out_specs=(block, block),
        compiler_params=params(12),
        cost_estimate=cost(4 << 20, 8 << 20),
        name="halves",
    )(wall)


def wall_kernel(arrived, high, low, message):
    x = arrived[0:32, :]
    for r in range(1, 8):
        x = x + arrived[r * 32 : (r + 1) * 32, :]
    x = block_transpose(x, 16)
    coeff = jnp.concatenate([x[g * 8 : (g + 1) * 8] for g in range(4)], 1)
    stacked = jnp.concatenate([p.astype(F32) for p in split(coeff)], 0).astype(BF16)
    response = jnp.zeros(coeff.shape, F32)
    owner = rows(coeff.shape) >> 1
    for i in range(4):
        a = dot(stacked, high[i], NT)
        b = dot(stacked, low[i], NT)
        response = jnp.where(owner == i, a[0:8] + (a[8:16] + b[0:8]), response)
    y = jnp.concatenate([response[:, g * 128 : (g + 1) * 128] for g in range(4)], 0)
    y = block_transpose(y, 16)
    for r in range(8):
        message[r * 32 : (r + 1) * 32, :] = y


def apply_wall(arrived, high, low):
    return pl.pallas_call(
        wall_kernel,
        out_shape=jax.ShapeDtypeStruct(arrived.shape, F32),
        in_specs=[VMEM, VMEM, VMEM],
        out_specs=VMEM,
        compiler_params=params(8),
        cost_estimate=cost(3 * 2 * 16 * 512 * 512 * 4, 4 << 20),
        name="wall",
    )(arrived, high, low)


def pack_kernel(mag, vel, left, right, bottom, top):
    nz, nr, cells = mag.shape[1:]
    lane = lanes((8, cells))
    for f in range(6):
        ref = mag if f < 3 else vel
        bottom[f] = ref[f % 3, 0]
        top[f] = ref[f % 3, nz - 1]

        def body(z, carry, ref=ref, f=f):
            low, high = carry
            for t in range(8):
                j = z * 8 + t
                tile = pltpu.roll(ref[f % 3, z, t * 8 : (t + 1) * 8, :], j, 1)
                low = jnp.where(lane == j, tile, low)
                high = jnp.where(lane == ((j + 127) & 127), tile, high)
            return low, high

        zero = jnp.zeros((8, cells), F32)
        low, high = lax.fori_loop(0, nz, body, (zero, zero))
        left[f] = low
        right[f] = high


def pack(mag, vel):
    nz, nr, cells = mag.shape[1:]
    edge = jax.ShapeDtypeStruct((6, 8, cells), F32)
    layer = jax.ShapeDtypeStruct((6, nr, cells), F32)
    return pl.pallas_call(
        pack_kernel,
        out_shape=(edge, edge, layer, layer),
        in_specs=[VMEM, VMEM],
        out_specs=(VMEM,) * 4,
        compiler_params=params(12),
        cost_estimate=cost(8 << 20, 4 << 20),
        name="pack",
    )(mag, vel)


def stencil_kernel(mag, vel, before, after, below, above, out, edge, pad_b, pad_u):
    nz, nr, cells = mag.shape[1:]
    lane = lanes((8, cells))
    row = rows((8, cells))
    inv_radial = 1.0 / (2.0 * RADIAL_STEP)
    inv_axial = 1.0 / (2.0 * AXIAL_STEP)
    angle_step = 2.0 * math.pi / (cells * 8)

    def body(z, _):
        for t in range(nr // 8):
            index = (t * 8 + row).astype(F32)
            radius = 1.0 - (nr - index - 0.5) * RADIAL_STEP
            inv_azimuth = 1.0 / (2.0 * radius * angle_step)
            inv_radius = 1.0 / radius
            second = 1.0 / (radius * angle_step) ** 2
            j = z * 8 + t
            grads = []
            centers = []
            extra = []
            for f in range(6):
                ref, pad, c = (mag, pad_b, f) if f < 3 else (vel, pad_u, f - 3)
                x = ref[c, z, t * 8 : (t + 1) * 8, :]
                outer = ref[c, z, min(t * 8 + 8, nr - 1) : min(t * 8 + 8, nr - 1) + 1, :]
                inner = ref[c, z, max(t * 8 - 1, 0) : max(t * 8 - 1, 0) + 1, :]
                r_next = jnp.where(row == 7, outer, pltpu.roll(x, 7, 0))
                r_prev = jnp.where(row == 0, inner, pltpu.roll(x, 1, 0))
                h_next = pltpu.roll(after[f], (255 - j) & 127, 1)
                h_prev = pltpu.roll(before[f], (129 - j) & 127, 1)
                p_next = jnp.where(lane == cells - 1, h_next, pltpu.roll(x, cells - 1, 1))
                p_prev = jnp.where(lane == 0, h_prev, pltpu.roll(x, 1, 1))
                z_next = pad[c, z + 2, t * 8 : (t + 1) * 8, :]
                z_prev = pad[c, z, t * 8 : (t + 1) * 8, :]
                centers.append(x)
                grads.append(
                    (
                        (r_next - r_prev) * inv_radial,
                        (p_next - p_prev) * inv_azimuth,
                        (z_next - z_prev) * inv_axial,
                    )
                )
                if f < 3:
                    twice = 2.0 * x
                    laplace = (r_next - twice + r_prev) * (1.0 / RADIAL_STEP**2)
                    laplace = laplace + grads[f][0] * inv_radius
                    laplace = laplace + (p_next - twice + p_prev) * second
                    laplace = laplace + (z_next - twice + z_prev) * (1.0 / AXIAL_STEP**2)
                    extra.append(laplace)
            for c in range(3):
                gb, gu = grads[c], grads[c + 3]
                carried = centers[3] * gb[0] + centers[4] * gb[1] + centers[5] * gb[2]
                stretched = centers[0] * gu[0] + centers[1] * gu[1] + centers[2] * gu[2]
                value = centers[c] + TIME_STEP * (DIFFUSIVITY * extra[c] - carried + stretched)
                out[c, z, t * 8 : (t + 1) * 8, :] = value
                if c and t == nr // 8 - 1:
                    edge[c - 1, z] = value
            if t == nr // 8 - 1:
                last = 1.0 - 0.5 * RADIAL_STEP
                fixed = TIME_STEP * DIFFUSIVITY * (1.0 / RADIAL_STEP**2 + inv_radial / last)
                edge[2, z] = fixed - (TIME_STEP * inv_radial) * centers[3]
        return 0

    for f in range(6):
        ref, pad, c = (mag, pad_b, f) if f < 3 else (vel, pad_u, f - 3)
        pad[c, 0] = below[f]
        pad[c, nz + 1] = above[f]
        pad[c, 1 : nz + 1] = ref[c]
    lax.fori_loop(0, nz, body, 0)


def stencil(mag, vel, before, after, below, above):
    nz, nr, cells = mag.shape[1:]
    return pl.pallas_call(
        stencil_kernel,
        out_shape=(
            jax.ShapeDtypeStruct(mag.shape, F32),
            jax.ShapeDtypeStruct((3, nz, 8, cells), F32),
        ),
        in_specs=[VMEM] * 6,
        out_specs=(VMEM, VMEM),
        scratch_shapes=[
            pltpu.VMEM((3, nz + 2, nr, cells), F32),
            pltpu.VMEM((3, nz + 2, nr, cells), F32),
        ],
        compiler_params=params(20),
        cost_estimate=cost(40 << 20, 8 << 20),
        name="stencil",
    )(mag, vel, before, after, below, above)


def decode_kernel(arrived, high, low, layers, edge, held, flux, out, fixed, sem):
    del held
    nz, cells = flux.shape[1:]
    turned = jnp.transpose(arrived[...], (1, 0))
    th, tl = split(turned)
    total = jnp.zeros((2 * nz, cells), F32)
    for i in range(4):
        part = slice(i * 2 * nz, (i + 1) * 2 * nz)
        total = total + dot3((th[part], tl[part]), (high[i], low[i]), NN)
    total = total.reshape(2, nz, cells)
    flux[...] = total
    thickness = layers[...].astype(F32) * (1.0 / LW)
    row = rows((nz, 8, cells))
    for c in range(2):
        change = (thickness * total[c])[:, None, :] * edge[2]
        fixed[c] = edge[c] - jnp.where(row == 7, change, 0.0)
    copy = pltpu.make_async_copy(fixed, out.at[1:3, :, 56:64, :], sem)
    copy.start()
    copy.wait()


def decode(arrived, high, low, layers, edge, held):
    nz, nr, cells = held.shape[1:]
    return pl.pallas_call(
        decode_kernel,
        out_shape=(
            jax.ShapeDtypeStruct((2, nz, cells), F32),
            jax.ShapeDtypeStruct(held.shape, F32),
        ),
        in_specs=[VMEM] * 5 + [ANY],
        out_specs=(VMEM, ANY),
        scratch_shapes=[pltpu.VMEM((2, nz, 8, cells), F32), pltpu.SemaphoreType.DMA],
        input_output_aliases={5: 1},
        compiler_params=params(8),
        cost_estimate=cost(12 << 20, 1 << 20),
        name="decode",
    )(arrived, high, low, layers.reshape(1, cells), edge, held)


def neighbours(low, high, axis, periodic):
    count = lax.axis_size(axis)
    forward = [(i, i + 1) for i in range(count - 1)]
    if periodic:
        forward.append((count - 1, 0))
    backward = [(target, source) for source, target in forward]
    return lax.ppermute(high, axis, forward), lax.ppermute(low, axis, backward)


def shards(magnetic, velocity, wall_response, mode_slots, wall_layers):
    message, table = encode(magnetic, mode_slots)
    arrived = lax.all_to_all(message, BOTH, 0, 0, tiled=True)
    left, right, bottom, top = pack(magnetic, velocity)
    before, after = neighbours(left, right, "region", True)
    below, above = neighbours(bottom, top, "slab", False)
    wall_high, wall_low = halves(wall_response)
    table_high, table_low = weigh(table, mode_slots)
    replies = apply_wall(arrived, wall_high, wall_low)
    returned = lax.all_to_all(replies, BOTH, 0, 0, tiled=True)
    stepped, edge = stencil(magnetic, velocity, before, after, below, above)
    wall_flux, magnetic_next = decode(
        returned, table_high, table_low, wall_layers, edge, stepped
    )
    return magnetic_next, wall_flux


def solution(mesh):
    placed = (
        P(None, "slab", None, "region"),
        P(None, "slab", None, "region"),
        P(BOTH, None, None),
        P(),
        P("region"),
    )
    return jax.shard_map(
        shards,
        mesh=mesh,
        in_specs=placed,
        out_specs=(P(None, "slab", None, "region"), P(None, "slab", "region")),
        check_vma=False,
    )
```

```python
import math

import jax
import jax.numpy as jnp
from jax import lax
from jax.experimental import pallas as pl
from jax.experimental.pallas import tpu as pltpu
from jax.sharding import PartitionSpec as P

LW = 8
TIME_STEP = 0.0003
DIFFUSIVITY = 0.001
RADIAL_STEP = 1.0 / 384.0
AXIAL_STEP = 1.0 / 768.0

F32 = jnp.float32
BF16 = jnp.bfloat16
BOTH = ("region", "slab")
VMEM = pl.BlockSpec(memory_space=pltpu.VMEM)
ANY = pl.BlockSpec(memory_space=pl.ANY)
HBM = pl.BlockSpec(memory_space=pltpu.HBM)
NT = (((1,), (1,)), ((), ()))
NN = (((1,), (0,)), ((), ()))


def pinned(*arrays):
    return [pltpu.with_memory_space_constraint(a, pltpu.HBM) for a in arrays]


def params(mib):
    return pltpu.CompilerParams(vmem_limit_bytes=mib * 1024 * 1024)


def cost(flops, nbytes):
    return pl.CostEstimate(flops=flops, bytes_accessed=nbytes, transcendentals=0)


def lanes(shape):
    return lax.broadcasted_iota(jnp.int32, shape, len(shape) - 1)


def rows(shape):
    return lax.broadcasted_iota(jnp.int32, shape, len(shape) - 2)


def split(x):
    high = x.astype(BF16)
    return high, (x - high.astype(F32)).astype(BF16)


def dot(a, b, dims):
    return lax.dot_general(a, b, dims, preferred_element_type=F32)


def half_turn_sine(phase, total):
    half = phase - total
    fold = jnp.abs(half)
    fold = jnp.minimum(fold, total - fold)
    x = fold.astype(F32) * (math.pi / total)
    y = x * x
    poly = -1.0 / math.factorial(11)
    for n, sign in ((9, 1.0), (7, -1.0), (5, 1.0), (3, -1.0)):
        poly = poly * y + sign / math.factorial(n)
    value = x + x * (y * poly)
    return jnp.where(half < 0, value, -value)


def block_transpose(x, width):
    r, b = rows(x.shape), lanes(x.shape) // width
    n, m = x.shape
    for bit in range(3):
        h = 1 << bit
        down = pltpu.roll(pltpu.roll(x, h, 0), m - width * h, 1)
        up = pltpu.roll(pltpu.roll(x, n - h, 0), width * h, 1)
        rb, bb = (r >> bit) & 1, (b >> bit) & 1
        x = jnp.where(rb == bb, x, jnp.where(rb == 1, down, up))
    return x


def encode_kernel(mag, modes, message, table, edge, slots, turned, parts, sems):
    count, cells = parts.shape[1], edge.shape[3]
    nmodes = 4 * count
    get_modes = pltpu.make_async_copy(modes, slots, sems.at[0])
    get_edge = pltpu.make_async_copy(mag.at[1:3, :, 56:64, :], edge, sems.at[1])
    get_modes.start()
    get_edge.start()
    first = lax.axis_index("region") * cells
    odd_cell = (2 * (first + lanes((cells, cells))) + 1).astype(F32)
    get_modes.wait()
    filler = jnp.zeros((120, 128), F32)
    turned[...] = jnp.transpose(jnp.concatenate([slots[...].astype(F32), filler], 0), (1, 0))
    for i in range(4):
        strip = turned[pl.ds(i, 32, stride=4), :]
        for half in range(count // 128):
            columns = [strip[:, half * 4 + q : half * 4 + q + 1] for q in range(4)]
            mode = jnp.concatenate([jnp.broadcast_to(c, (32, cells)) for c in columns], 0)
            mode = mode.astype(jnp.int32)
            phase = (((mode + 1) >> 1).astype(F32) * odd_cell).astype(jnp.int32)
            phase = jnp.where((mode & 1) == 1, phase, phase + nmodes // 2) & (2 * nmodes - 1)
            high, low = split(half_turn_sine(phase, nmodes))
            part = slice(half * 128, half * 128 + 128)
            parts[i, part, 0:cells] = high
            parts[i, part, cells : 2 * cells] = low
    put_table = pltpu.make_async_copy(parts, table, sems.at[2])
    put_table.start()
    get_edge.wait()
    trace = edge[:, :, 7, :].reshape(32, cells)
    high, low = split(jnp.concatenate([trace] * 4, 0))
    weights = jnp.concatenate([jnp.concatenate([p, p], 1) for p in (high, low)], 0)
    lane = lanes((count, 128)) // 32
    out = jnp.zeros((count, 128), F32)
    for i in range(4):
        strip = turned[pl.ds(i, 32, stride=4), :]
        single = (strip == 0.0) | (strip == float(nmodes - 1))
        strip = jnp.where(single, 1.0 / nmodes, 2.0 / nmodes)
        scale = [jnp.broadcast_to(strip[:, r : r + 1], (32, 128)) for r in range(count // 32)]
        both = dot(parts[i], weights, NT)
        both = (both[:, 0:128] + both[:, 128:256]) * jnp.concatenate(scale, 0)
        out = jnp.where(lane == i, both, out)
    message[...] = out
    put_table.wait()


def encode(mag, modes):
    nz, _, cells = mag.shape[1:]
    count = modes.size // 4
    return pl.pallas_call(
        encode_kernel,
        out_shape=(
            jax.ShapeDtypeStruct((count, 128), F32),
            pltpu.HBM((4, count, 2 * cells), BF16),
        ),
        in_specs=[HBM, HBM],
        out_specs=(VMEM, HBM),
        scratch_shapes=[
            pltpu.VMEM((2, nz, 8, cells), F32),
            pltpu.VMEM((8, 128), jnp.int32),
            pltpu.VMEM((128, 128), F32),
            pltpu.VMEM((4, count, 2 * cells), BF16),
            pltpu.SemaphoreType.DMA((3,)),
        ],
        compiler_params=params(8),
        cost_estimate=cost(3 * 2 * 1024 * 128 * 128, 1 << 20),
        name="encode",
    )(*pinned(mag, modes.reshape(8, 128)))


def wall_kernel(arrived, wall, *rest):
    message, held, sems = rest[-3:]
    copies = [pltpu.make_async_copy(wall.at[i], held.at[i], sems.at[i]) for i in range(4)]
    for copy in copies:
        copy.start()
    x = arrived[0:32, :]
    for r in range(1, 8):
        x = x + arrived[r * 32 : (r + 1) * 32, :]
    x = block_transpose(x, 16)
    coeff = jnp.concatenate([x[g * 8 : (g + 1) * 8] for g in range(4)], 1)
    stacked = jnp.concatenate([p.astype(F32) for p in split(coeff)], 0).astype(BF16)
    response = jnp.zeros(coeff.shape, F32)
    owner = rows(coeff.shape) >> 1
    for i in range(4):
        copies[i].wait()
        high, low = split(held[i])
        a = dot(stacked, high, NT)
        b = dot(stacked, low, NT)
        response = jnp.where(owner == i, a[0:8] + (a[8:16] + b[0:8]), response)
    y = jnp.concatenate([response[:, g * 128 : (g + 1) * 128] for g in range(4)], 0)
    y = block_transpose(y, 16)
    for r in range(8):
        message[r * 32 : (r + 1) * 32, :] = y


def apply_wall(arrived, wall, *earlier):
    return pl.pallas_call(
        wall_kernel,
        out_shape=jax.ShapeDtypeStruct(arrived.shape, F32),
        in_specs=[VMEM, HBM] + [ANY] * len(earlier),
        out_specs=VMEM,
        scratch_shapes=[pltpu.VMEM(wall.shape, F32), pltpu.SemaphoreType.DMA((4,))],
        compiler_params=params(16),
        cost_estimate=cost(3 * 2 * 16 * 512 * 512 * 4, 4 << 20),
        name="wall",
    )(arrived, *pinned(wall), *earlier)


def fetch(mag, vel, held, sems):
    return [
        [
            pltpu.make_async_copy(
                ref.at[:, pl.ds(part * 4, 4)], held.at[k, :, pl.ds(part * 4, 4)], sems.at[k, part]
            )
            for k, ref in enumerate((mag, vel))
        ]
        for part in range(held.shape[2] // 4)
    ]


def pack_kernel(mag, vel, left, right, bottom, top, held, low_sems, high_sems, sems):
    nz, nr, cells = mag.shape[1:]
    lane = lanes((8, cells))
    copies = fetch(mag, vel, held, sems)
    for pair in copies:
        for copy in pair:
            copy.start()

    def body(z, carry):
        low, high = list(carry[0]), list(carry[1])
        for t in range(8):
            j = z * 8 + t
            here, wrapped = lane == j, lane == ((j + 127) & 127)
            for f in range(6):
                tile = pltpu.roll(held[f // 3, f % 3, z, t * 8 : (t + 1) * 8, :], j, 1)
                low[f] = jnp.where(here, tile, low[f])
                high[f] = jnp.where(wrapped, tile, high[f])
        return tuple(low), tuple(high)

    zero = (jnp.zeros((8, cells), F32),) * 6
    carry = (zero, zero)
    ends = []
    for part, pair in enumerate(copies):
        for copy in pair:
            copy.wait()
        for k in range(2):
            if part == 0:
                ends.append(pltpu.make_async_copy(held.at[k, :, 0], bottom.at[pl.ds(3 * k, 3)], low_sems.at[k]))
                ends[-1].start()
            if part == nz // 4 - 1:
                ends.append(pltpu.make_async_copy(held.at[k, :, nz - 1], top.at[pl.ds(3 * k, 3)], high_sems.at[k]))
                ends[-1].start()
        carry = lax.fori_loop(part * 4, part * 4 + 4, body, carry)
    for f in range(6):
        left[f] = carry[0][f]
        right[f] = carry[1][f]
    for copy in ends:
        copy.wait()


def pack(mag, vel):
    nz, nr, cells = mag.shape[1:]
    edge = jax.ShapeDtypeStruct((6, 8, cells), F32)
    return pl.pallas_call(
        pack_kernel,
        out_shape=(edge, edge, pltpu.HBM((6, nr, cells), F32), pltpu.HBM((6, nr, cells), F32)),
        in_specs=[HBM, HBM],
        out_specs=(VMEM, VMEM, HBM, HBM),
        scratch_shapes=[
            pltpu.VMEM((2, *mag.shape), F32),
            pltpu.SemaphoreType.DMA((2,)),
            pltpu.SemaphoreType.DMA((2,)),
            pltpu.SemaphoreType.DMA((2, nz // 4)),
        ],
        compiler_params=params(12),
        cost_estimate=cost(8 << 20, 4 << 20),
        name="pack",
    )(*pinned(mag, vel))


def stencil_kernel(mag, vel, before, after, below, above, out, held, stepped, factors, gets, sems):
    nz, nr, cells = mag.shape[1:]
    lane = lanes((8, cells))
    row = rows((8, cells))
    copies = fetch(mag, vel, held, gets)
    for pair in copies:
        for copy in pair:
            copy.start()
    angle_step = 2.0 * math.pi / (cells * 8)
    spread = TIME_STEP * DIFFUSIVITY
    by_radial = TIME_STEP / (2.0 * RADIAL_STEP)
    by_axial = TIME_STEP / (2.0 * AXIAL_STEP)
    second_radial = spread / RADIAL_STEP**2
    second_axial = spread / AXIAL_STEP**2
    for t in range(nr // 8):
        radius = 1.0 - (nr - (t * 8 + row).astype(F32) - 0.5) * RADIAL_STEP
        arc = 1.0 / (radius * angle_step)
        second = spread * arc * arc
        factors[0, t] = (0.5 * TIME_STEP) * arc
        factors[1, t] = (spread / (2.0 * RADIAL_STEP)) / radius
        factors[2, t] = second
        factors[3, t] = 1.0 - 2.0 * (second + (second_radial + second_axial))

    def layer(z, down, up):
        for t in range(nr // 8):
            j = z * 8 + t
            rows8 = slice(t * 8, t * 8 + 8)
            x, dr, dp, dz, sr, sp, sz = [], [], [], [], [], [], []
            for f in range(6):
                ref, c = held.at[f // 3], f % 3
                here = ref[c, z, rows8, :]
                if t == 0:
                    inner = jnp.where(row == 0, here, pltpu.roll(here, 1, 0))
                else:
                    inner = ref[c, z, t * 8 - 1 : t * 8 + 7, :]
                if t == nr // 8 - 1:
                    outer = jnp.where(row == 7, here, pltpu.roll(here, 7, 0))
                else:
                    outer = ref[c, z, t * 8 + 1 : t * 8 + 9, :]
                far = pltpu.roll(after[f], (255 - j) & 127, 1)
                near = pltpu.roll(before[f], (129 - j) & 127, 1)
                p_next = jnp.where(lane == cells - 1, far, pltpu.roll(here, cells - 1, 1))
                p_prev = jnp.where(lane == 0, near, pltpu.roll(here, 1, 1))
                z_next = up(f, rows8)
                z_prev = down(f, rows8)
                x.append(here)
                dr.append(outer - inner)
                dp.append(p_next - p_prev)
                dz.append(z_next - z_prev)
                if f < 3:
                    sr.append(outer + inner)
                    sp.append(p_next + p_prev)
                    sz.append(z_next + z_prev)
            turn, curve, second, keep = (factors[n, t] for n in range(4))
            ur = curve - by_radial * x[3]
            up_ = turn * x[4]
            uz = by_axial * x[5]
            br = by_radial * x[0]
            bp = turn * x[1]
            bz = by_axial * x[2]
            for c in range(3):
                value = keep * x[c] + second_radial * sr[c] + (second * sp[c] + second_axial * sz[c])
                value = value + (ur * dr[c] - up_ * dp[c]) - uz * dz[c]
                value = value + (br * dr[c + 3] + bp * dp[c + 3]) + bz * dz[c + 3]
                stepped[c, z, rows8, :] = value

    def inside(z, step):
        return lambda f, rows8: held[f // 3, f % 3, z + step, rows8, :]

    def send(part):
        return pltpu.make_async_copy(
            stepped.at[:, pl.ds(part * 4, 4)], out.at[:, pl.ds(part * 4, 4)], sems.at[part]
        )

    def body(z, _):
        layer(z, inside(z, -1), inside(z, 1))
        return 0

    parts = nz // 4
    for copy in copies[0]:
        copy.wait()
    layer(0, lambda f, rows8: below[f, rows8, :], inside(0, 1))
    for part in range(parts):
        if part < parts - 1:
            for copy in copies[part + 1]:
                copy.wait()
        lax.fori_loop(max(part * 4, 1), min(part * 4 + 4, nz - 1), body, 0)
        if part == parts - 1:
            layer(nz - 1, inside(nz - 1, -1), lambda f, rows8: above[f, rows8, :])
        send(part).start()
    for part in range(parts):
        send(part).wait()


def stencil(mag, vel, before, after, below, above):
    nz, nr, cells = mag.shape[1:]
    return pl.pallas_call(
        stencil_kernel,
        out_shape=pltpu.HBM(mag.shape, F32),
        in_specs=[HBM] * 2 + [VMEM] * 4,
        out_specs=HBM,
        scratch_shapes=[
            pltpu.VMEM((2, *mag.shape), F32),
            pltpu.VMEM(mag.shape, F32),
            pltpu.VMEM((4, nr // 8, 8, cells), F32),
            pltpu.SemaphoreType.DMA((2, nz // 4)),
            pltpu.SemaphoreType.DMA((nz // 4,)),
        ],
        compiler_params=params(16),
        cost_estimate=cost(40 << 20, 8 << 20),
        name="stencil",
    )(*pinned(mag, vel), before, after, below, above)


def decode_kernel(arrived, table, layers, vel, held, flux, out, parts, edge, wind, sems):
    nz, cells = flux.shape[1:]
    get_table = pltpu.make_async_copy(table, parts, sems.at[3])
    get_table.start()
    get_edge = pltpu.make_async_copy(held.at[1:3, :, 56:64, :], edge, sems.at[0])
    get_wind = pltpu.make_async_copy(vel.at[0, :, 56:64, :], wind, sems.at[1])
    get_edge.start()
    get_wind.start()
    high, low = split(jnp.transpose(arrived[...], (1, 0)))
    total = jnp.zeros((4 * nz, 2 * cells), F32)
    get_table.wait()
    for i in range(4):
        part = slice(i * 2 * nz, (i + 1) * 2 * nz)
        pair = jnp.concatenate([high[part], low[part]], 0)
        total = total + dot(pair, parts[i], NN)
    total = total[:, 0:cells] + total[:, cells : 2 * cells]
    total = (total[0 : 2 * nz] + total[2 * nz : 4 * nz]).reshape(2, nz, cells)
    flux[...] = total
    thickness = layers[...].astype(F32) * (1.0 / LW)
    by_radial = TIME_STEP / (2.0 * RADIAL_STEP)
    last = 1.0 - 0.5 * RADIAL_STEP
    fixed = TIME_STEP * DIFFUSIVITY / RADIAL_STEP**2 + DIFFUSIVITY * by_radial / last
    row = rows((nz, 8, cells))
    get_wind.wait()
    factor = jnp.where(row == 7, fixed - by_radial * wind[...], 0.0)
    get_edge.wait()
    for c in range(2):
        edge[c] = edge[c] - (thickness * total[c])[:, None, :] * factor
    put = pltpu.make_async_copy(edge, out.at[1:3, :, 56:64, :], sems.at[2])
    put.start()
    put.wait()


def decode(arrived, table, layers, vel, held):
    nz, nr, cells = held.shape[1:]
    return pl.pallas_call(
        decode_kernel,
        out_shape=(
            jax.ShapeDtypeStruct((2, nz, cells), F32),
            pltpu.HBM(held.shape, F32),
        ),
        in_specs=[VMEM, HBM, VMEM, HBM, HBM],
        out_specs=(VMEM, HBM),
        scratch_shapes=[
            pltpu.VMEM(table.shape, BF16),
            pltpu.VMEM((2, nz, 8, cells), F32),
            pltpu.VMEM((nz, 8, cells), F32),
            pltpu.SemaphoreType.DMA((4,)),
        ],
        input_output_aliases={4: 1},
        compiler_params=params(8),
        cost_estimate=cost(12 << 20, 1 << 20),
        name="decode",
    )(arrived, *pinned(table), layers.reshape(1, cells), *pinned(vel, held))


def neighbours(low, high, axis, periodic):
    count = lax.axis_size(axis)
    forward = [(i, i + 1) for i in range(count - 1)]
    if periodic:
        forward.append((count - 1, 0))
    backward = [(target, source) for source, target in forward]
    return lax.ppermute(high, axis, forward), lax.ppermute(low, axis, backward)


def shards(magnetic, velocity, wall_response, mode_slots, wall_layers):
    message, table = encode(magnetic, mode_slots)
    arrived = lax.all_to_all(message, BOTH, 0, 0, tiled=True)
    left, right, bottom, top = pack(magnetic, velocity)
    before, after = neighbours(left, right, "region", True)
    below, above = neighbours(bottom, top, "slab", False)
    replies = apply_wall(arrived, wall_response, before, after, below, above)
    returned = lax.all_to_all(replies, BOTH, 0, 0, tiled=True)
    stepped = stencil(magnetic, velocity, before, after, below, above)
    wall_flux, magnetic_next = decode(returned, table, wall_layers, velocity, stepped)
    return magnetic_next, wall_flux


def solution(mesh):
    placed = (
        P(None, "slab", None, "region"),
        P(None, "slab", None, "region"),
        P(BOTH, None, None),
        P(),
        P("region"),
    )
    return jax.shard_map(
        shards,
        mesh=mesh,
        in_specs=placed,
        out_specs=(P(None, "slab", None, "region"), P(None, "slab", "region")),
        check_vma=False,
    )
```

```python
import math

import jax
import jax.numpy as jnp
from jax import lax
from jax.experimental import pallas as pl
from jax.experimental.pallas import tpu as pltpu
from jax.sharding import PartitionSpec as P

LW = 8
TIME_STEP = 0.0003
DIFFUSIVITY = 0.001
RADIAL_STEP = 1.0 / 384.0
AXIAL_STEP = 1.0 / 768.0

F32 = jnp.float32
BF16 = jnp.bfloat16
BOTH = ("region", "slab")
VMEM = pl.BlockSpec(memory_space=pltpu.VMEM)
ANY = pl.BlockSpec(memory_space=pl.ANY)
HBM = pl.BlockSpec(memory_space=pltpu.HBM)
NT = (((1,), (1,)), ((), ()))
NN = (((1,), (0,)), ((), ()))


def pinned(*arrays):
    return [pltpu.with_memory_space_constraint(a, pltpu.HBM) for a in arrays]


def resident(*arrays):
    return [pltpu.with_memory_space_constraint(a, pltpu.VMEM) for a in arrays]


def params(mib):
    return pltpu.CompilerParams(vmem_limit_bytes=mib * 1024 * 1024)


def cost(flops, nbytes):
    return pl.CostEstimate(flops=flops, bytes_accessed=nbytes, transcendentals=0)


def lanes(shape):
    return lax.broadcasted_iota(jnp.int32, shape, len(shape) - 1)


def rows(shape):
    return lax.broadcasted_iota(jnp.int32, shape, len(shape) - 2)


def split(x):
    high = x.astype(BF16)
    return high, (x - high.astype(F32)).astype(BF16)


def dot(a, b, dims):
    return lax.dot_general(a, b, dims, preferred_element_type=F32)


def half_turn_sine(phase, total):
    half = phase - total
    fold = jnp.abs(half)
    fold = jnp.minimum(fold, total - fold)
    x = fold.astype(F32) * (math.pi / total)
    y = x * x
    poly = -1.0 / math.factorial(11)
    for n, sign in ((9, 1.0), (7, -1.0), (5, 1.0), (3, -1.0)):
        poly = poly * y + sign / math.factorial(n)
    value = x + x * (y * poly)
    return jnp.where(half < 0, value, -value)


def block_transpose(x, width):
    r, b = rows(x.shape), lanes(x.shape) // width
    n, m = x.shape
    for bit in range(3):
        h = 1 << bit
        down = pltpu.roll(pltpu.roll(x, h, 0), m - width * h, 1)
        up = pltpu.roll(pltpu.roll(x, n - h, 0), width * h, 1)
        rb, bb = (r >> bit) & 1, (b >> bit) & 1
        x = jnp.where(rb == bb, x, jnp.where(rb == 1, down, up))
    return x


def encode_kernel(mag, vel, modes, message, parts, ends_a, ends_b, edge, slots, turned, sems, end_sems):
    count, cells = parts.shape[1], edge.shape[3]
    nmodes = 4 * count
    get_modes = pltpu.make_async_copy(modes, slots, sems.at[0])
    get_edge = pltpu.make_async_copy(mag.at[1:3, :, 56:64, :], edge, sems.at[1])
    get_modes.start()
    get_edge.start()
    odd = lax.axis_index("slab") % 2
    last = mag.shape[1] - 1
    ends = []
    for k, ref in enumerate((mag, vel)):
        for n, (target, layer) in enumerate(((ends_a, last * (1 - odd)), (ends_b, last * odd))):
            ends.append(
                pltpu.make_async_copy(ref.at[:, layer], target.at[pl.ds(3 * k, 3)], end_sems.at[k, n])
            )
            ends[-1].start()
    first = lax.axis_index("region") * cells
    odd_cell = (2 * (first + lanes((cells, cells))) + 1).astype(F32)
    get_modes.wait()
    filler = jnp.zeros((120, 128), F32)
    turned[...] = jnp.transpose(jnp.concatenate([slots[...].astype(F32), filler], 0), (1, 0))
    for i in range(4):
        strip = turned[pl.ds(i, 32, stride=4), :]
        for half in range(count // 128):
            columns = [strip[:, half * 4 + q : half * 4 + q + 1] for q in range(4)]
            mode = jnp.concatenate([jnp.broadcast_to(c, (32, cells)) for c in columns], 0)
            mode = mode.astype(jnp.int32)
            phase = (((mode + 1) >> 1).astype(F32) * odd_cell).astype(jnp.int32)
            phase = jnp.where((mode & 1) == 1, phase, phase + nmodes // 2) & (2 * nmodes - 1)
            high, low = split(half_turn_sine(phase, nmodes))
            part = slice(half * 128, half * 128 + 128)
            parts[i, part, 0:cells] = high
            parts[i, part, cells : 2 * cells] = low
    get_edge.wait()
    trace = edge[:, :, 7, :].reshape(32, cells)
    high, low = split(jnp.concatenate([trace] * 4, 0))
    weights = jnp.concatenate([jnp.concatenate([p, p], 1) for p in (high, low)], 0)
    lane = lanes((count, 128)) // 32
    out = jnp.zeros((count, 128), F32)
    for i in range(4):
        strip = turned[pl.ds(i, 32, stride=4), :]
        single = (strip == 0.0) | (strip == float(nmodes - 1))
        strip = jnp.where(single, 1.0 / nmodes, 2.0 / nmodes)
        scale = [jnp.broadcast_to(strip[:, r : r + 1], (32, 128)) for r in range(count // 32)]
        both = dot(parts[i], weights, NT)
        both = (both[:, 0:128] + both[:, 128:256]) * jnp.concatenate(scale, 0)
        out = jnp.where(lane == i, both, out)
    message[...] = out
    for copy in ends:
        copy.wait()


def encode(mag, vel, modes):
    nz, nr, cells = mag.shape[1:]
    count = modes.size // 4
    layer = pltpu.VMEM((6, nr, cells), F32)
    return pl.pallas_call(
        encode_kernel,
        out_shape=(
            jax.ShapeDtypeStruct((count, 128), F32),
            pltpu.VMEM((4, count, 2 * cells), BF16),
            layer,
            layer,
        ),
        in_specs=[HBM, HBM, HBM],
        out_specs=(VMEM,) * 4,
        scratch_shapes=[
            pltpu.VMEM((2, nz, 8, cells), F32),
            pltpu.VMEM((8, 128), jnp.int32),
            pltpu.VMEM((128, 128), F32),
            pltpu.SemaphoreType.DMA((2,)),
            pltpu.SemaphoreType.DMA((2, 2)),
        ],
        compiler_params=params(8),
        cost_estimate=cost(3 * 2 * 1024 * 128 * 128, 1 << 20),
        name="encode",
    )(*pinned(mag, vel, modes.reshape(8, 128)))


def wall_kernel(arrived, near, wall, *rest):
    message, held, sems = rest[-3:]
    count = near.shape[0]
    copies = [pltpu.make_async_copy(wall.at[count + i], held.at[i], sems.at[i]) for i in range(held.shape[0])]
    for copy in copies:
        copy.start()
    x = arrived[0:32, :]
    for r in range(1, 8):
        x = x + arrived[r * 32 : (r + 1) * 32, :]
    x = block_transpose(x, 16)
    coeff = jnp.concatenate([x[g * 8 : (g + 1) * 8] for g in range(4)], 1)
    stacked = jnp.concatenate([p.astype(F32) for p in split(coeff)], 0).astype(BF16)
    response = jnp.zeros(coeff.shape, F32)
    owner = rows(coeff.shape) >> 1
    for i in range(4):
        if i < count:
            high, low = split(near[i])
        else:
            copies[i - count].wait()
            high, low = split(held[i - count])
        a = dot(stacked, high, NT)
        b = dot(stacked, low, NT)
        response = jnp.where(owner == i, a[0:8] + (a[8:16] + b[0:8]), response)
    y = jnp.concatenate([response[:, g * 128 : (g + 1) * 128] for g in range(4)], 0)
    y = block_transpose(y, 16)
    for r in range(8):
        message[r * 32 : (r + 1) * 32, :] = y


def apply_wall(arrived, near, wall, *earlier):
    return pl.pallas_call(
        wall_kernel,
        out_shape=jax.ShapeDtypeStruct(arrived.shape, F32),
        in_specs=[VMEM, VMEM, HBM] + [ANY] * len(earlier),
        out_specs=VMEM,
        scratch_shapes=[
            pltpu.VMEM((wall.shape[0] - near.shape[0], *wall.shape[1:]), F32),
            pltpu.SemaphoreType.DMA((wall.shape[0] - near.shape[0],)),
        ],
        compiler_params=params(16),
        cost_estimate=cost(3 * 2 * 16 * 512 * 512 * 4, 4 << 20),
        name="wall",
    )(arrived, *resident(near), *pinned(wall), *earlier)


def fetch(mag, vel, held, sems):
    return [
        [
            pltpu.make_async_copy(
                ref.at[:, pl.ds(part * 4, 4)], held.at[k, :, pl.ds(part * 4, 4)], sems.at[k, part]
            )
            for k, ref in enumerate((mag, vel))
        ]
        for part in range(held.shape[2] // 4)
    ]


def pack_kernel(mag, vel, wall, ends_a, ends_b, near_wall, held, sems, wall_sem):
    nz, nr, cells = mag.shape[1:]
    lane = lanes((8, cells))
    copies = fetch(mag, vel, held, sems)
    for pair in copies:
        for copy in pair:
            copy.start()
    get_wall = pltpu.make_async_copy(wall.at[pl.ds(0, near_wall.shape[0])], near_wall, wall_sem)
    get_wall.start()

    def body(z, carry):
        low, high = list(carry[0]), list(carry[1])
        for t in range(8):
            j = z * 8 + t
            here, wrapped = lane == j, lane == ((j + 127) & 127)
            for f in range(6):
                tile = pltpu.roll(held[f // 3, f % 3, z, t * 8 : (t + 1) * 8, :], j, 1)
                low[f] = jnp.where(here, tile, low[f])
                high[f] = jnp.where(wrapped, tile, high[f])
        return tuple(low), tuple(high)

    zero = (jnp.zeros((8, cells), F32),) * 6
    carry = (zero, zero)
    for part, pair in enumerate(copies):
        for copy in pair:
            copy.wait()
        carry = lax.fori_loop(part * 4, part * 4 + 4, body, carry)
    even = lax.axis_index("region") % 2 == 0
    for f in range(6):
        low, high = carry[0][f], carry[1][f]
        ends_a[f] = jnp.where(even, high, low)
        ends_b[f] = jnp.where(even, low, high)
    get_wall.wait()


def pack(mag, vel, wall):
    nz, nr, cells = mag.shape[1:]
    edge = pltpu.VMEM((6, 8, cells), F32)
    return pl.pallas_call(
        pack_kernel,
        out_shape=(edge, edge, pltpu.VMEM((2, *wall.shape[1:]), F32)),
        in_specs=[HBM, HBM, HBM],
        out_specs=(VMEM, VMEM, VMEM),
        scratch_shapes=[
            pltpu.VMEM((2, *mag.shape), F32),
            pltpu.SemaphoreType.DMA((2, nz // 4)),
            pltpu.SemaphoreType.DMA,
        ],
        compiler_params=params(12),
        cost_estimate=cost(8 << 20, 4 << 20),
        name="pack",
    )(*pinned(mag, vel, wall))


def stencil_kernel(mag, vel, side_a, side_b, end_a, end_b, out, edge, held, stepped, factors, sides, gets, sems):
    nz, nr, cells = mag.shape[1:]
    lane = lanes((8, cells))
    row = rows((8, cells))
    copies = fetch(mag, vel, held, gets)
    for pair in copies:
        for copy in pair:
            copy.start()
    even = lax.axis_index("region") % 2 == 0
    sides[0] = jnp.where(even, side_b[...], side_a[...])
    sides[1] = jnp.where(even, side_a[...], side_b[...])
    even_slab = lax.axis_index("slab") % 2 == 0
    angle_step = 2.0 * math.pi / (cells * 8)
    spread = TIME_STEP * DIFFUSIVITY
    by_radial = TIME_STEP / (2.0 * RADIAL_STEP)
    by_axial = TIME_STEP / (2.0 * AXIAL_STEP)
    second_radial = spread / RADIAL_STEP**2
    second_axial = spread / AXIAL_STEP**2
    for t in range(nr // 8):
        radius = 1.0 - (nr - (t * 8 + row).astype(F32) - 0.5) * RADIAL_STEP
        arc = 1.0 / (radius * angle_step)
        second = spread * arc * arc
        factors[0, t] = (0.5 * TIME_STEP) * arc
        factors[1, t] = (spread / (2.0 * RADIAL_STEP)) / radius
        factors[2, t] = second
        factors[3, t] = 1.0 - 2.0 * (second + (second_radial + second_axial))

    def layer(z, down, up):
        for t in range(nr // 8):
            j = z * 8 + t
            rows8 = slice(t * 8, t * 8 + 8)
            x, dr, dp, dz, sr, sp, sz = [], [], [], [], [], [], []
            for f in range(6):
                ref, c = held.at[f // 3], f % 3
                here = ref[c, z, rows8, :]
                if t == 0:
                    inner = jnp.where(row == 0, here, pltpu.roll(here, 1, 0))
                else:
                    inner = ref[c, z, t * 8 - 1 : t * 8 + 7, :]
                if t == nr // 8 - 1:
                    outer = jnp.where(row == 7, here, pltpu.roll(here, 7, 0))
                else:
                    outer = ref[c, z, t * 8 + 1 : t * 8 + 9, :]
                far = pltpu.roll(sides[1, f], (255 - j) & 127, 1)
                near = pltpu.roll(sides[0, f], (129 - j) & 127, 1)
                p_next = jnp.where(lane == cells - 1, far, pltpu.roll(here, cells - 1, 1))
                p_prev = jnp.where(lane == 0, near, pltpu.roll(here, 1, 1))
                z_next = up(f, rows8)
                z_prev = down(f, rows8)
                x.append(here)
                dr.append(outer - inner)
                dp.append(p_next - p_prev)
                dz.append(z_next - z_prev)
                if f < 3:
                    sr.append(outer + inner)
                    sp.append(p_next + p_prev)
                    sz.append(z_next + z_prev)
            turn, curve, second, keep = (factors[n, t] for n in range(4))
            ur = curve - by_radial * x[3]
            up_ = turn * x[4]
            uz = by_axial * x[5]
            br = by_radial * x[0]
            bp = turn * x[1]
            bz = by_axial * x[2]
            for c in range(3):
                value = keep * x[c] + second_radial * sr[c] + (second * sp[c] + second_axial * sz[c])
                value = value + (ur * dr[c] - up_ * dp[c]) - uz * dz[c]
                value = value + (br * dr[c + 3] + bp * dp[c + 3]) + bz * dz[c + 3]
                stepped[c, z, rows8, :] = value
                if c and t == nr // 8 - 1:
                    edge[c - 1, z] = value
            if t == nr // 8 - 1:
                at_wall = second_radial + spread / (2.0 * RADIAL_STEP) / (1.0 - 0.5 * RADIAL_STEP)
                edge[2, z] = jnp.where(row == 7, at_wall - by_radial * x[3], 0.0)

    def inside(z, step):
        return lambda f, rows8: held[f // 3, f % 3, z + step, rows8, :]

    def send(part):
        return pltpu.make_async_copy(
            stepped.at[:, pl.ds(part * 4, 4)], out.at[:, pl.ds(part * 4, 4)], sems.at[part]
        )

    def body(z, _):
        layer(z, inside(z, -1), inside(z, 1))
        return 0

    parts = nz // 4
    for copy in copies[0]:
        copy.wait()
    layer(0, lambda f, rows8: jnp.where(even_slab, end_b[f, rows8, :], end_a[f, rows8, :]), inside(0, 1))
    for part in range(parts):
        if part < parts - 1:
            for copy in copies[part + 1]:
                copy.wait()
        lax.fori_loop(max(part * 4, 1), min(part * 4 + 4, nz - 1), body, 0)
        if part == parts - 1:
            layer(nz - 1, inside(nz - 1, -1), lambda f, rows8: jnp.where(even_slab, end_a[f, rows8, :], end_b[f, rows8, :]))
        send(part).start()
    for part in range(parts):
        send(part).wait()


def stencil(mag, vel, *halos):
    nz, nr, cells = mag.shape[1:]
    return pl.pallas_call(
        stencil_kernel,
        out_shape=(pltpu.HBM(mag.shape, F32), pltpu.VMEM((3, nz, 8, cells), F32)),
        in_specs=[HBM] * 2 + [VMEM] * 4,
        out_specs=(HBM, VMEM),
        scratch_shapes=[
            pltpu.VMEM((2, *mag.shape), F32),
            pltpu.VMEM(mag.shape, F32),
            pltpu.VMEM((4, nr // 8, 8, cells), F32),
            pltpu.VMEM((2, 6, 8, cells), F32),
            pltpu.SemaphoreType.DMA((2, nz // 4)),
            pltpu.SemaphoreType.DMA((nz // 4,)),
        ],
        compiler_params=params(16),
        cost_estimate=cost(40 << 20, 8 << 20),
        name="stencil",
    )(*pinned(mag, vel), *halos)


def decode_kernel(arrived, table, layers, edge, held, flux, out, fixed, sem):
    del held
    nz, cells = flux.shape[1:]
    high, low = split(jnp.transpose(arrived[...], (1, 0)))
    total = jnp.zeros((4 * nz, 2 * cells), F32)
    for i in range(4):
        part = slice(i * 2 * nz, (i + 1) * 2 * nz)
        pair = jnp.concatenate([high[part], low[part]], 0)
        total = total + dot(pair, table[i], NN)
    total = total[:, 0:cells] + total[:, cells : 2 * cells]
    total = (total[0 : 2 * nz] + total[2 * nz : 4 * nz]).reshape(2, nz, cells)
    thickness = layers[...].astype(F32) * (1.0 / LW)
    for c in range(2):
        fixed[c] = edge[c] - (thickness * total[c])[:, None, :] * edge[2]
    put = pltpu.make_async_copy(fixed, out.at[1:3, :, 56:64, :], sem)
    put.start()
    flux[...] = total
    put.wait()


def decode(arrived, table, layers, edge, held):
    nz, nr, cells = held.shape[1:]
    return pl.pallas_call(
        decode_kernel,
        out_shape=(
            jax.ShapeDtypeStruct((2, nz, cells), F32),
            pltpu.HBM(held.shape, F32),
        ),
        in_specs=[VMEM, VMEM, VMEM, VMEM, HBM],
        out_specs=(VMEM, HBM),
        scratch_shapes=[pltpu.VMEM((2, nz, 8, cells), F32), pltpu.SemaphoreType.DMA],
        input_output_aliases={4: 1},
        compiler_params=params(8),
        cost_estimate=cost(12 << 20, 1 << 20),
        name="decode",
    )(arrived, *resident(table), layers.reshape(1, cells), *resident(edge), *pinned(held))


def swap(payload, axis, offset, periodic):
    count = lax.axis_size(axis)
    pairs = []
    for i in range(offset, count - 1 + offset, 2):
        j = i + 1
        if j < count or periodic:
            pairs += [(i, j % count), (j % count, i)]
    return lax.ppermute(payload, axis, pairs)


def shards(magnetic, velocity, wall_response, mode_slots, wall_layers):
    message, table, ends_a, ends_b = encode(magnetic, velocity, mode_slots)
    arrived = lax.all_to_all(message, BOTH, 0, 0, tiled=True)
    end_b = swap(ends_b, "slab", 1, False)
    sides_a, sides_b, near = pack(magnetic, velocity, wall_response)
    side_b = swap(sides_b, "region", 1, True)
    side_a = swap(sides_a, "region", 0, True)
    end_a = swap(ends_a, "slab", 0, False)
    replies = apply_wall(arrived, near, wall_response, side_a, side_b, end_a, end_b)
    returned = lax.all_to_all(replies, BOTH, 0, 0, tiled=True)
    stepped, edge = stencil(magnetic, velocity, side_a, side_b, end_a, end_b)
    wall_flux, magnetic_next = decode(returned, table, wall_layers, edge, stepped)
    return magnetic_next, wall_flux


def solution(mesh):
    placed = (
        P(None, "slab", None, "region"),
        P(None, "slab", None, "region"),
        P(BOTH, None, None),
        P(),
        P("region"),
    )
    return jax.shard_map(
        shards,
        mesh=mesh,
        in_specs=placed,
        out_specs=(P(None, "slab", None, "region"), P(None, "slab", "region")),
        check_vma=False,
    )
```

```python
import math

import jax
import jax.numpy as jnp
from jax import lax
from jax.experimental import pallas as pl
from jax.experimental.pallas import tpu as pltpu
from jax.sharding import PartitionSpec as P

LW = 8
TIME_STEP = 0.0003
DIFFUSIVITY = 0.001
RADIAL_STEP = 1.0 / 384.0
AXIAL_STEP = 1.0 / 768.0

F32 = jnp.float32
BF16 = jnp.bfloat16
BOTH = ("region", "slab")
VMEM = pl.BlockSpec(memory_space=pltpu.VMEM)
ANY = pl.BlockSpec(memory_space=pl.ANY)
HBM = pl.BlockSpec(memory_space=pltpu.HBM)
NT = (((1,), (1,)), ((), ()))
NN = (((1,), (0,)), ((), ()))


def pinned(*arrays):
    return [pltpu.with_memory_space_constraint(a, pltpu.HBM) for a in arrays]


def resident(*arrays):
    return [pltpu.with_memory_space_constraint(a, pltpu.VMEM) for a in arrays]


def params(mib):
    return pltpu.CompilerParams(vmem_limit_bytes=mib * 1024 * 1024)


def cost(flops, nbytes):
    return pl.CostEstimate(flops=flops, bytes_accessed=nbytes, transcendentals=0)


def lanes(shape):
    return lax.broadcasted_iota(jnp.int32, shape, len(shape) - 1)


def rows(shape):
    return lax.broadcasted_iota(jnp.int32, shape, len(shape) - 2)


def split(x):
    high = x.astype(BF16)
    return high, (x - high.astype(F32)).astype(BF16)


def dot(a, b, dims):
    return lax.dot_general(a, b, dims, preferred_element_type=F32)


def half_turn_sine(phase, total):
    half = phase - total
    fold = jnp.abs(half)
    fold = jnp.minimum(fold, total - fold)
    x = fold.astype(F32) * (math.pi / total)
    y = x * x
    poly = -1.0 / math.factorial(11)
    for n, sign in ((9, 1.0), (7, -1.0), (5, 1.0), (3, -1.0)):
        poly = poly * y + sign / math.factorial(n)
    value = x + x * (y * poly)
    return jnp.where(half < 0, value, -value)


def block_transpose(x, width):
    r, b = rows(x.shape), lanes(x.shape) // width
    n, m = x.shape
    for bit in range(3):
        h = 1 << bit
        down = pltpu.roll(pltpu.roll(x, h, 0), m - width * h, 1)
        up = pltpu.roll(pltpu.roll(x, n - h, 0), width * h, 1)
        rb, bb = (r >> bit) & 1, (b >> bit) & 1
        x = jnp.where(rb == bb, x, jnp.where(rb == 1, down, up))
    return x


def encode_kernel(mag, vel, modes, wall, message, parts, ends_a, ends_b, near, edge, slots, turned, sems, end_sems):
    count, cells = parts.shape[1], edge.shape[3]
    nmodes = 4 * count
    get_modes = pltpu.make_async_copy(modes, slots, sems.at[0])
    get_edge = pltpu.make_async_copy(mag.at[1:3, :, 56:64, :], edge, sems.at[1])
    get_modes.start()
    get_edge.start()
    odd = lax.axis_index("slab") % 2
    last = mag.shape[1] - 1
    ends = []
    for k, ref in enumerate((mag, vel)):
        for n, (target, layer) in enumerate(((ends_a, last * (1 - odd)), (ends_b, last * odd))):
            ends.append(
                pltpu.make_async_copy(ref.at[:, layer], target.at[pl.ds(3 * k, 3)], end_sems.at[k, n])
            )
            ends[-1].start()
    ends.append(pltpu.make_async_copy(wall.at[pl.ds(0, near.shape[0])], near, sems.at[2]))
    ends[-1].start()
    first = lax.axis_index("region") * cells
    odd_cell = (2 * (first + lanes((cells, cells))) + 1).astype(F32)
    get_modes.wait()
    filler = jnp.zeros((120, 128), F32)
    turned[...] = jnp.transpose(jnp.concatenate([slots[...].astype(F32), filler], 0), (1, 0))
    for i in range(4):
        strip = turned[pl.ds(i, 32, stride=4), :]
        for half in range(count // 128):
            columns = [strip[:, half * 4 + q : half * 4 + q + 1] for q in range(4)]
            mode = jnp.concatenate([jnp.broadcast_to(c, (32, cells)) for c in columns], 0)
            mode = mode.astype(jnp.int32)
            phase = (((mode + 1) >> 1).astype(F32) * odd_cell).astype(jnp.int32)
            phase = jnp.where((mode & 1) == 1, phase, phase + nmodes // 2) & (2 * nmodes - 1)
            high, low = split(half_turn_sine(phase, nmodes))
            part = slice(half * 128, half * 128 + 128)
            parts[i, part, 0:cells] = high
            parts[i, part, cells : 2 * cells] = low
    get_edge.wait()
    trace = edge[:, :, 7, :].reshape(32, cells)
    high, low = split(jnp.concatenate([trace] * 4, 0))
    weights = jnp.concatenate([jnp.concatenate([p, p], 1) for p in (high, low)], 0)
    lane = lanes((count, 128)) // 32
    out = jnp.zeros((count, 128), F32)
    for i in range(4):
        strip = turned[pl.ds(i, 32, stride=4), :]
        single = (strip == 0.0) | (strip == float(nmodes - 1))
        strip = jnp.where(single, 1.0 / nmodes, 2.0 / nmodes)
        scale = [jnp.broadcast_to(strip[:, r : r + 1], (32, 128)) for r in range(count // 32)]
        both = dot(parts[i], weights, NT)
        both = (both[:, 0:128] + both[:, 128:256]) * jnp.concatenate(scale, 0)
        out = jnp.where(lane == i, both, out)
    message[...] = out
    for copy in ends:
        copy.wait()


def encode(mag, vel, modes, wall):
    nz, nr, cells = mag.shape[1:]
    count = modes.size // 4
    layer = pltpu.VMEM((6, nr, cells), F32)
    return pl.pallas_call(
        encode_kernel,
        out_shape=(
            jax.ShapeDtypeStruct((count, 128), F32),
            pltpu.VMEM((4, count, 2 * cells), BF16),
            layer,
            layer,
            pltpu.VMEM((2, *wall.shape[1:]), F32),
        ),
        in_specs=[HBM] * 4,
        out_specs=(VMEM,) * 5,
        scratch_shapes=[
            pltpu.VMEM((2, nz, 8, cells), F32),
            pltpu.VMEM((8, 128), jnp.int32),
            pltpu.VMEM((128, 128), F32),
            pltpu.SemaphoreType.DMA((3,)),
            pltpu.SemaphoreType.DMA((2, 2)),
        ],
        compiler_params=params(8),
        cost_estimate=cost(3 * 2 * 1024 * 128 * 128, 1 << 20),
        name="encode",
    )(*pinned(mag, vel, modes.reshape(8, 128), wall))


def wall_kernel(arrived, near, wall, *rest):
    message, held, sems = rest[-3:]
    count = near.shape[0]
    copies = [pltpu.make_async_copy(wall.at[count + i], held.at[i], sems.at[i]) for i in range(held.shape[0])]
    for copy in copies:
        copy.start()
    x = arrived[0:32, :]
    for r in range(1, 8):
        x = x + arrived[r * 32 : (r + 1) * 32, :]
    x = block_transpose(x, 16)
    coeff = jnp.concatenate([x[g * 8 : (g + 1) * 8] for g in range(4)], 1)
    stacked = jnp.concatenate([p.astype(F32) for p in split(coeff)], 0).astype(BF16)
    response = jnp.zeros(coeff.shape, F32)
    owner = rows(coeff.shape) >> 1
    for i in range(4):
        if i < count:
            high, low = split(near[i])
        else:
            copies[i - count].wait()
            high, low = split(held[i - count])
        a = dot(stacked, high, NT)
        b = dot(stacked, low, NT)
        response = jnp.where(owner == i, a[0:8] + (a[8:16] + b[0:8]), response)
    y = jnp.concatenate([response[:, g * 128 : (g + 1) * 128] for g in range(4)], 0)
    y = block_transpose(y, 16)
    for r in range(8):
        message[r * 32 : (r + 1) * 32, :] = y


def apply_wall(arrived, near, wall, *earlier):
    return pl.pallas_call(
        wall_kernel,
        out_shape=jax.ShapeDtypeStruct(arrived.shape, F32),
        in_specs=[VMEM, VMEM, HBM] + [ANY] * len(earlier),
        out_specs=VMEM,
        scratch_shapes=[
            pltpu.VMEM((wall.shape[0] - near.shape[0], *wall.shape[1:]), F32),
            pltpu.SemaphoreType.DMA((wall.shape[0] - near.shape[0],)),
        ],
        compiler_params=params(16),
        cost_estimate=cost(1 << 10, 1 << 10),
        name="wall",
    )(arrived, *resident(near), *pinned(wall), *earlier)


def fetch(mag, vel, held, sems):
    return [
        [
            pltpu.make_async_copy(
                ref.at[:, pl.ds(part * 4, 4)], held.at[k, :, pl.ds(part * 4, 4)], sems.at[k, part]
            )
            for k, ref in enumerate((mag, vel))
        ]
        for part in range(held.shape[2] // 4)
    ]


def pack_kernel(mag, vel, sides, held, sems):
    nz, nr, cells = mag.shape[1:]
    lane = lanes((8, cells))
    copies = fetch(mag, vel, held, sems)
    for pair in copies:
        for copy in pair:
            copy.start()

    def body(z, carry):
        out = list(carry)
        for t in range(8):
            j = 2 * ((z & 7) * 8 + t)
            here = (lane == j) | (lane == ((j + 127) & 127))
            for f in range(6):
                tile = pltpu.roll(held[f // 3, f % 3, z, t * 8 : (t + 1) * 8, :], j, 1)
                out[f] = jnp.where(here, tile, out[f])
        return tuple(out)

    for part, pair in enumerate(copies):
        for copy in pair:
            copy.wait()
        if part % 2 == 0:
            carry = (jnp.zeros((8, cells), F32),) * 6
        carry = lax.fori_loop(part * 4, part * 4 + 4, body, carry)
        if part % 2 == 1:
            for f in range(6):
                sides[f, part // 2] = carry[f]


def pack(mag, vel):
    nz, nr, cells = mag.shape[1:]
    return pl.pallas_call(
        pack_kernel,
        out_shape=pltpu.VMEM((6, 2, 8, cells), F32),
        in_specs=[HBM, HBM],
        out_specs=VMEM,
        scratch_shapes=[
            pltpu.VMEM((2, *mag.shape), F32),
            pltpu.SemaphoreType.DMA((2, nz // 4)),
        ],
        compiler_params=params(12),
        cost_estimate=cost(8 << 20, 4 << 20),
        name="pack",
    )(*pinned(mag, vel))


def stencil_kernel(mag, vel, side_a, side_b, end_a, end_b, out, edge, held, stepped, factors, sides, gets, sems):
    nz, nr, cells = mag.shape[1:]
    lane = lanes((8, cells))
    row = rows((8, cells))
    copies = fetch(mag, vel, held, gets)
    for pair in copies:
        for copy in pair:
            copy.start()
    even = lax.axis_index("region") % 2 == 0
    for f in range(6):
        for half in range(2):
            a, b = side_a[f, half], side_b[f, half]
            low = pltpu.roll(jnp.where(even, b, a), 1, 1)
            high = pltpu.roll(jnp.where(even, a, b), cells - 1, 1)
            sides[f, half] = jnp.where(lane % 2 == 0, low, high)
    even_slab = lax.axis_index("slab") % 2 == 0
    angle_step = 2.0 * math.pi / (cells * 8)
    spread = TIME_STEP * DIFFUSIVITY
    by_radial = TIME_STEP / (2.0 * RADIAL_STEP)
    by_axial = TIME_STEP / (2.0 * AXIAL_STEP)
    second_radial = spread / RADIAL_STEP**2
    second_axial = spread / AXIAL_STEP**2
    for t in range(nr // 8):
        radius = 1.0 - (nr - (t * 8 + row).astype(F32) - 0.5) * RADIAL_STEP
        arc = 1.0 / (radius * angle_step)
        second = spread * arc * arc
        factors[0, t] = (0.5 * TIME_STEP) * arc
        factors[1, t] = (spread / (2.0 * RADIAL_STEP)) / radius
        factors[2, t] = second
        factors[3, t] = 1.0 - 2.0 * (second + (second_radial + second_axial))

    def layer(z, down, up):
        for t in range(nr // 8):
            j = (z & 7) * 8 + t
            rows8 = slice(t * 8, t * 8 + 8)
            x, dr, dp, dz, sr, sp, sz = [], [], [], [], [], [], []
            for f in range(6):
                ref, c = held.at[f // 3], f % 3
                here = ref[c, z, rows8, :]
                if t == 0:
                    inner = jnp.where(row == 0, here, pltpu.roll(here, 1, 0))
                else:
                    inner = ref[c, z, t * 8 - 1 : t * 8 + 7, :]
                if t == nr // 8 - 1:
                    outer = jnp.where(row == 7, here, pltpu.roll(here, 7, 0))
                else:
                    outer = ref[c, z, t * 8 + 1 : t * 8 + 9, :]
                beyond = pltpu.roll(sides[f, z >> 3], (256 - 2 * j) & 127, 1)
                p_next = jnp.where(lane == cells - 1, beyond, pltpu.roll(here, cells - 1, 1))
                p_prev = jnp.where(lane == 0, beyond, pltpu.roll(here, 1, 1))
                z_next = up(f, rows8)
                z_prev = down(f, rows8)
                x.append(here)
                dr.append(outer - inner)
                dp.append(p_next - p_prev)
                dz.append(z_next - z_prev)
                if f < 3:
                    sr.append(outer + inner)
                    sp.append(p_next + p_prev)
                    sz.append(z_next + z_prev)
            turn, curve, second, keep = (factors[n, t] for n in range(4))
            ur = curve - by_radial * x[3]
            up_ = turn * x[4]
            uz = by_axial * x[5]
            br = by_radial * x[0]
            bp = turn * x[1]
            bz = by_axial * x[2]
            for c in range(3):
                value = keep * x[c] + second_radial * sr[c] + (second * sp[c] + second_axial * sz[c])
                value = value + (ur * dr[c] - up_ * dp[c]) - uz * dz[c]
                value = value + (br * dr[c + 3] + bp * dp[c + 3]) + bz * dz[c + 3]
                stepped[c, z, rows8, :] = value
                if c and t == nr // 8 - 1:
                    edge[c - 1, z] = value
            if t == nr // 8 - 1:
                at_wall = second_radial + spread / (2.0 * RADIAL_STEP) / (1.0 - 0.5 * RADIAL_STEP)
                edge[2, z] = jnp.where(row == 7, at_wall - by_radial * x[3], 0.0)

    def inside(z, step):
        return lambda f, rows8: held[f // 3, f % 3, z + step, rows8, :]

    def send(part):
        return pltpu.make_async_copy(
            stepped.at[:, pl.ds(part * 4, 4)], out.at[:, pl.ds(part * 4, 4)], sems.at[part]
        )

    def body(z, _):
        layer(z, inside(z, -1), inside(z, 1))
        return 0

    parts = nz // 4
    for copy in copies[0]:
        copy.wait()
    layer(0, lambda f, rows8: jnp.where(even_slab, end_b[f, rows8, :], end_a[f, rows8, :]), inside(0, 1))
    for part in range(parts):
        if part < parts - 1:
            for copy in copies[part + 1]:
                copy.wait()
        lax.fori_loop(max(part * 4, 1), min(part * 4 + 4, nz - 1), body, 0)
        if part == parts - 1:
            layer(nz - 1, inside(nz - 1, -1), lambda f, rows8: jnp.where(even_slab, end_a[f, rows8, :], end_b[f, rows8, :]))
        send(part).start()
    for part in range(parts):
        send(part).wait()


def stencil(mag, vel, *halos):
    nz, nr, cells = mag.shape[1:]
    return pl.pallas_call(
        stencil_kernel,
        out_shape=(pltpu.HBM(mag.shape, F32), pltpu.VMEM((3, nz, 8, cells), F32)),
        in_specs=[HBM] * 2 + [VMEM] * 4,
        out_specs=(HBM, VMEM),
        scratch_shapes=[
            pltpu.VMEM((2, *mag.shape), F32),
            pltpu.VMEM(mag.shape, F32),
            pltpu.VMEM((4, nr // 8, 8, cells), F32),
            pltpu.VMEM((6, 2, 8, cells), F32),
            pltpu.SemaphoreType.DMA((2, nz // 4)),
            pltpu.SemaphoreType.DMA((nz // 4,)),
        ],
        compiler_params=params(16),
        cost_estimate=cost(40 << 30, 8 << 30),
        name="stencil",
    )(*pinned(mag, vel), *halos)


def decode_kernel(arrived, table, layers, edge, held, flux, out, fixed, sem):
    del held
    nz, cells = flux.shape[1:]
    high, low = split(jnp.transpose(arrived[...], (1, 0)))
    total = jnp.zeros((4 * nz, 2 * cells), F32)
    for i in range(4):
        part = slice(i * 2 * nz, (i + 1) * 2 * nz)
        pair = jnp.concatenate([high[part], low[part]], 0)
        total = total + dot(pair, table[i], NN)
    total = total[:, 0:cells] + total[:, cells : 2 * cells]
    total = (total[0 : 2 * nz] + total[2 * nz : 4 * nz]).reshape(2, nz, cells)
    thickness = layers[...].astype(F32) * (1.0 / LW)
    for c in range(2):
        fixed[c] = edge[c] - (thickness * total[c])[:, None, :] * edge[2]
    put = pltpu.make_async_copy(fixed, out.at[1:3, :, 56:64, :], sem)
    put.start()
    flux[...] = total
    put.wait()


def decode(arrived, table, layers, edge, held):
    nz, nr, cells = held.shape[1:]
    return pl.pallas_call(
        decode_kernel,
        out_shape=(
            jax.ShapeDtypeStruct((2, nz, cells), F32),
            pltpu.HBM(held.shape, F32),
        ),
        in_specs=[VMEM, VMEM, VMEM, VMEM, HBM],
        out_specs=(VMEM, HBM),
        scratch_shapes=[pltpu.VMEM((2, nz, 8, cells), F32), pltpu.SemaphoreType.DMA],
        input_output_aliases={4: 1},
        compiler_params=params(8),
        cost_estimate=cost(12 << 20, 1 << 20),
        name="decode",
    )(arrived, *resident(table), layers.reshape(1, cells), *resident(edge), *pinned(held))


def swap(payload, axis, offset, periodic):
    count = lax.axis_size(axis)
    pairs = []
    for i in range(offset, count - 1 + offset, 2):
        j = i + 1
        if j < count or periodic:
            pairs += [(i, j % count), (j % count, i)]
    return lax.ppermute(payload, axis, pairs)


def shards(magnetic, velocity, wall_response, mode_slots, wall_layers):
    message, table, ends_a, ends_b, near = encode(magnetic, velocity, mode_slots, wall_response)
    arrived = lax.all_to_all(message, BOTH, 0, 0, tiled=True)
    end_b = swap(ends_b, "slab", 1, False)
    sides = pack(magnetic, velocity)
    side_b = swap(sides, "region", 1, True)
    side_a = swap(sides, "region", 0, True)
    end_a = swap(ends_a, "slab", 0, False)
    replies = apply_wall(arrived, near, wall_response, sides)
    returned = lax.all_to_all(replies, BOTH, 0, 0, tiled=True)
    stepped, edge = stencil(magnetic, velocity, side_a, side_b, end_a, end_b)
    wall_flux, magnetic_next = decode(returned, table, wall_layers, edge, stepped)
    return magnetic_next, wall_flux


def solution(mesh):
    placed = (
        P(None, "slab", None, "region"),
        P(None, "slab", None, "region"),
        P(BOTH, None, None),
        P(),
        P("region"),
    )
    return jax.shard_map(
        shards,
        mesh=mesh,
        in_specs=placed,
        out_specs=(P(None, "slab", None, "region"), P(None, "slab", "region")),
        check_vma=False,
    )
```

```python
import math

import jax
import jax.numpy as jnp
from jax import lax
from jax.experimental import pallas as pl
from jax.experimental.pallas import tpu as pltpu
from jax.sharding import PartitionSpec as P

LW = 8
TIME_STEP = 0.0003
DIFFUSIVITY = 0.001
RADIAL_STEP = 1.0 / 384.0
AXIAL_STEP = 1.0 / 768.0

F32 = jnp.float32
BF16 = jnp.bfloat16
BOTH = ("region", "slab")
VMEM = pl.BlockSpec(memory_space=pltpu.VMEM)
ANY = pl.BlockSpec(memory_space=pl.ANY)
HBM = pl.BlockSpec(memory_space=pltpu.HBM)
NT = (((1,), (1,)), ((), ()))
NN = (((1,), (0,)), ((), ()))


def pinned(*arrays):
    return [pltpu.with_memory_space_constraint(a, pltpu.HBM) for a in arrays]


def resident(*arrays):
    return [pltpu.with_memory_space_constraint(a, pltpu.VMEM) for a in arrays]


def params(mib):
    return pltpu.CompilerParams(vmem_limit_bytes=mib * 1024 * 1024)


def cost(flops, nbytes):
    return pl.CostEstimate(flops=flops, bytes_accessed=nbytes, transcendentals=0)


def lanes(shape):
    return lax.broadcasted_iota(jnp.int32, shape, len(shape) - 1)


def rows(shape):
    return lax.broadcasted_iota(jnp.int32, shape, len(shape) - 2)


def split(x):
    high = x.astype(BF16)
    return high, (x - high.astype(F32)).astype(BF16)


def dot(a, b, dims):
    return lax.dot_general(a, b, dims, preferred_element_type=F32)


def half_turn_sine(phase, total):
    half = phase - total
    fold = jnp.abs(half)
    fold = jnp.minimum(fold, total - fold)
    x = fold.astype(F32) * (math.pi / total)
    y = x * x
    poly = -1.0 / math.factorial(11)
    for n, sign in ((9, 1.0), (7, -1.0), (5, 1.0), (3, -1.0)):
        poly = poly * y + sign / math.factorial(n)
    value = x + x * (y * poly)
    return jnp.where(half < 0, value, -value)


def block_transpose(x, width):
    r, b = rows(x.shape), lanes(x.shape) // width
    n, m = x.shape
    for bit in range(3):
        h = 1 << bit
        down = pltpu.roll(pltpu.roll(x, h, 0), m - width * h, 1)
        up = pltpu.roll(pltpu.roll(x, n - h, 0), width * h, 1)
        rb, bb = (r >> bit) & 1, (b >> bit) & 1
        x = jnp.where(rb == bb, x, jnp.where(rb == 1, down, up))
    return x


def encode_kernel(mag, vel, modes, wall, message, parts, ends_a, ends_b, near, edge, slots, turned, sems, end_sems):
    count, cells = parts.shape[1], edge.shape[3]
    nmodes = 4 * count
    get_modes = pltpu.make_async_copy(modes, slots, sems.at[0])
    get_edge = pltpu.make_async_copy(mag.at[1:3, :, 56:64, :], edge, sems.at[1])
    get_modes.start()
    get_edge.start()
    odd = lax.axis_index("slab") % 2
    last = mag.shape[1] - 1
    ends = []
    for k, ref in enumerate((mag, vel)):
        for n, (target, layer) in enumerate(((ends_a, last * (1 - odd)), (ends_b, last * odd))):
            ends.append(
                pltpu.make_async_copy(ref.at[:, layer], target.at[pl.ds(3 * k, 3)], end_sems.at[k, n])
            )
            ends[-1].start()
    ends.append(pltpu.make_async_copy(wall.at[pl.ds(0, near.shape[0])], near, sems.at[2]))
    ends[-1].start()
    first = lax.axis_index("region") * cells
    odd_cell = (2 * (first + lanes((cells, cells))) + 1).astype(F32)
    get_modes.wait()
    filler = jnp.zeros((120, 128), F32)
    turned[...] = jnp.transpose(jnp.concatenate([slots[...].astype(F32), filler], 0), (1, 0))
    for i in range(4):
        strip = turned[pl.ds(i, 32, stride=4), :]
        for half in range(count // 128):
            columns = [strip[:, half * 4 + q : half * 4 + q + 1] for q in range(4)]
            mode = jnp.concatenate([jnp.broadcast_to(c, (32, cells)) for c in columns], 0)
            mode = mode.astype(jnp.int32)
            phase = (((mode + 1) >> 1).astype(F32) * odd_cell).astype(jnp.int32)
            phase = jnp.where((mode & 1) == 1, phase, phase + nmodes // 2) & (2 * nmodes - 1)
            high, low = split(half_turn_sine(phase, nmodes))
            part = slice(half * 128, half * 128 + 128)
            parts[i, part, 0:cells] = high
            parts[i, part, cells : 2 * cells] = low
    get_edge.wait()
    trace = edge[:, :, 7, :].reshape(32, cells)
    high, low = split(jnp.concatenate([trace] * 4, 0))
    weights = jnp.concatenate([jnp.concatenate([p, p], 1) for p in (high, low)], 0)
    lane = lanes((count, 128)) // 32
    out = jnp.zeros((count, 128), F32)
    for i in range(4):
        strip = turned[pl.ds(i, 32, stride=4), :]
        single = (strip == 0.0) | (strip == float(nmodes - 1))
        strip = jnp.where(single, 1.0 / nmodes, 2.0 / nmodes)
        scale = [jnp.broadcast_to(strip[:, r : r + 1], (32, 128)) for r in range(count // 32)]
        both = dot(parts[i], weights, NT)
        both = (both[:, 0:128] + both[:, 128:256]) * jnp.concatenate(scale, 0)
        out = jnp.where(lane == i, both, out)
    message[...] = out
    for copy in ends:
        copy.wait()


def encode(mag, vel, modes, wall):
    nz, nr, cells = mag.shape[1:]
    count = modes.size // 4
    layer = pltpu.VMEM((6, nr, cells), F32)
    return pl.pallas_call(
        encode_kernel,
        out_shape=(
            jax.ShapeDtypeStruct((count, 128), F32),
            pltpu.VMEM((4, count, 2 * cells), BF16),
            layer,
            layer,
            pltpu.VMEM((2, *wall.shape[1:]), F32),
        ),
        in_specs=[HBM] * 4,
        out_specs=(VMEM,) * 5,
        scratch_shapes=[
            pltpu.VMEM((2, nz, 8, cells), F32),
            pltpu.VMEM((8, 128), jnp.int32),
            pltpu.VMEM((128, 128), F32),
            pltpu.SemaphoreType.DMA((3,)),
            pltpu.SemaphoreType.DMA((2, 2)),
        ],
        compiler_params=params(8),
        cost_estimate=cost(3 * 2 * 1024 * 128 * 128, 1 << 20),
        name="encode",
    )(*pinned(mag, vel, modes.reshape(8, 128), wall))


def wall_kernel(arrived, near, wall, message, held, sems):
    count = near.shape[0]
    copies = [pltpu.make_async_copy(wall.at[count + i], held.at[i], sems.at[i]) for i in range(held.shape[0])]
    for copy in copies:
        copy.start()
    x = arrived[0:32, :]
    for r in range(1, 8):
        x = x + arrived[r * 32 : (r + 1) * 32, :]
    x = block_transpose(x, 16)
    coeff = jnp.concatenate([x[g * 8 : (g + 1) * 8] for g in range(4)], 1)
    stacked = jnp.concatenate([p.astype(F32) for p in split(coeff)], 0).astype(BF16)
    response = jnp.zeros(coeff.shape, F32)
    owner = rows(coeff.shape) >> 1
    for i in range(4):
        if i < count:
            high, low = split(near[i])
        else:
            copies[i - count].wait()
            high, low = split(held[i - count])
        a = dot(stacked, high, NT)
        b = dot(stacked, low, NT)
        response = jnp.where(owner == i, a[0:8] + (a[8:16] + b[0:8]), response)
    y = jnp.concatenate([response[:, g * 128 : (g + 1) * 128] for g in range(4)], 0)
    y = block_transpose(y, 16)
    for r in range(8):
        message[r * 32 : (r + 1) * 32, :] = y


def apply_wall(arrived, near, wall):
    return pl.pallas_call(
        wall_kernel,
        out_shape=jax.ShapeDtypeStruct(arrived.shape, F32),
        in_specs=[VMEM, VMEM, HBM],
        out_specs=VMEM,
        scratch_shapes=[
            pltpu.VMEM((wall.shape[0] - near.shape[0], *wall.shape[1:]), F32),
            pltpu.SemaphoreType.DMA((wall.shape[0] - near.shape[0],)),
        ],
        compiler_params=params(16),
        cost_estimate=cost(1 << 10, 1 << 10),
        name="wall",
    )(arrived, *resident(near), *pinned(wall))


def fetch(mag, vel, first, held, sems):
    return [
        [
            pltpu.make_async_copy(
                ref.at[:, pl.ds(first + part * 4, 4)], held.at[k, :, pl.ds(part * 4, 4)], sems.at[k, part]
            )
            for k, ref in enumerate((mag, vel))
        ]
        for part in range(held.shape[2] // 4)
    ]


def pack_kernel(mag, vel, earlier, sides, kept, held, kept_sems, held_sems):
    del earlier
    nz, nr, cells = mag.shape[1:]
    lane = lanes((8, cells))
    halves = ((kept, fetch(mag, vel, 0, kept, kept_sems)), (held, fetch(mag, vel, nz // 2, held, held_sems)))
    for _, copies in halves:
        for pair in copies:
            for copy in pair:
                copy.start()
    for half, (ref, copies) in enumerate(halves):
        out = [jnp.zeros((8, cells), F32)] * 6
        for z in range(nz // 2):
            if z % 4 == 0:
                for copy in copies[z // 4]:
                    copy.wait()
            for t in range(8):
                j = 2 * (z * 8 + t)
                here = (lane == j) | (lane == ((j + 127) & 127))
                for f in range(6):
                    tile = pltpu.roll(ref[f // 3, f % 3, z, t * 8 : (t + 1) * 8, :], j, 1)
                    out[f] = jnp.where(here, tile, out[f])
        for f in range(6):
            sides[f, half] = out[f]


def pack(mag, vel, earlier):
    nz, nr, cells = mag.shape[1:]
    return pl.pallas_call(
        pack_kernel,
        out_shape=(pltpu.VMEM((6, 2, 8, cells), F32), pltpu.VMEM((2, 3, nz // 2, nr, cells), F32)),
        in_specs=[HBM, HBM, ANY],
        out_specs=(VMEM, VMEM),
        scratch_shapes=[
            pltpu.VMEM((2, 3, nz // 2, nr, cells), F32),
            pltpu.SemaphoreType.DMA((2, nz // 8)),
            pltpu.SemaphoreType.DMA((2, nz // 8)),
        ],
        compiler_params=params(12),
        cost_estimate=cost(40 << 30, 8 << 30),
        name="pack",
    )(*pinned(mag, vel), earlier)


def stencil_kernel(mag, vel, kept, side_a, side_b, end_a, end_b, out, edge, held, stepped, factors, sides, gets, sems):
    nz, nr, cells = mag.shape[1:]
    lane = lanes((8, cells))
    row = rows((8, cells))
    copies = fetch(mag, vel, nz // 2, held, gets)
    for pair in copies:
        for copy in pair:
            copy.start()
    even = lax.axis_index("region") % 2 == 0
    for f in range(6):
        for half in range(2):
            a, b = side_a[f, half], side_b[f, half]
            low = pltpu.roll(jnp.where(even, b, a), 1, 1)
            high = pltpu.roll(jnp.where(even, a, b), cells - 1, 1)
            sides[f, half] = jnp.where(lane % 2 == 0, low, high)
    even_slab = lax.axis_index("slab") % 2 == 0
    angle_step = 2.0 * math.pi / (cells * 8)
    spread = TIME_STEP * DIFFUSIVITY
    by_radial = TIME_STEP / (2.0 * RADIAL_STEP)
    by_axial = TIME_STEP / (2.0 * AXIAL_STEP)
    second_radial = spread / RADIAL_STEP**2
    second_axial = spread / AXIAL_STEP**2
    for t in range(nr // 8):
        radius = 1.0 - (nr - (t * 8 + row).astype(F32) - 0.5) * RADIAL_STEP
        arc = 1.0 / (radius * angle_step)
        second = spread * arc * arc
        factors[0, t] = (0.5 * TIME_STEP) * arc
        factors[1, t] = (spread / (2.0 * RADIAL_STEP)) / radius
        factors[2, t] = second
        factors[3, t] = 1.0 - 2.0 * (second + (second_radial + second_axial))

    def layer(z, down, up):
        field, place = whose(z)
        for t in range(nr // 8):
            j = (z & 7) * 8 + t
            rows8 = slice(t * 8, t * 8 + 8)
            x, dr, dp, dz, sr, sp, sz = [], [], [], [], [], [], []
            for f in range(6):
                ref, c = field.at[f // 3, f % 3], place
                here = ref[c, rows8, :]
                if t == 0:
                    inner = jnp.where(row == 0, here, pltpu.roll(here, 1, 0))
                else:
                    inner = ref[c, t * 8 - 1 : t * 8 + 7, :]
                if t == nr // 8 - 1:
                    outer = jnp.where(row == 7, here, pltpu.roll(here, 7, 0))
                else:
                    outer = ref[c, t * 8 + 1 : t * 8 + 9, :]
                beyond = pltpu.roll(sides[f, z >> 3], (256 - 2 * j) & 127, 1)
                p_next = jnp.where(lane == cells - 1, beyond, pltpu.roll(here, cells - 1, 1))
                p_prev = jnp.where(lane == 0, beyond, pltpu.roll(here, 1, 1))
                z_next = up(f, rows8)
                z_prev = down(f, rows8)
                x.append(here)
                dr.append(outer - inner)
                dp.append(p_next - p_prev)
                dz.append(z_next - z_prev)
                if f < 3:
                    sr.append(outer + inner)
                    sp.append(p_next + p_prev)
                    sz.append(z_next + z_prev)
            turn, curve, second, keep = (factors[n, t] for n in range(4))
            ur = curve - by_radial * x[3]
            up_ = turn * x[4]
            uz = by_axial * x[5]
            br = by_radial * x[0]
            bp = turn * x[1]
            bz = by_axial * x[2]
            for c in range(3):
                value = keep * x[c] + second_radial * sr[c] + (second * sp[c] + second_axial * sz[c])
                value = value + (ur * dr[c] - up_ * dp[c]) - uz * dz[c]
                value = value + (br * dr[c + 3] + bp * dp[c + 3]) + bz * dz[c + 3]
                stepped[c, z, rows8, :] = value
                if c and t == nr // 8 - 1:
                    edge[c - 1, z] = value
            if t == nr // 8 - 1:
                at_wall = second_radial + spread / (2.0 * RADIAL_STEP) / (1.0 - 0.5 * RADIAL_STEP)
                edge[2, z] = jnp.where(row == 7, at_wall - by_radial * x[3], 0.0)

    def inside(z, step):
        field, place = whose(z, step)
        return lambda f, rows8: field[f // 3, f % 3, place, rows8, :]

    def send(n, first, count):
        part = pl.ds(first, count)
        return pltpu.make_async_copy(stepped.at[:, part], out.at[:, part], sems.at[n])

    def whose(z, step=0):
        if isinstance(z, int):
            return (kept, z + step) if z + step < nz // 2 else (held, z + step - nz // 2)
        return (kept, z + step) if in_kept[0] else (held, z + step - nz // 2)

    def body(z, _):
        layer(z, inside(z, -1), inside(z, 1))
        return 0

    in_kept = [True]
    sends = []
    for n, (first, count) in enumerate(((0, 4), (4, 4), (8, 4), (12, 2), (14, 2))):
        if first == nz // 2:
            in_kept[0] = False
        begin, end = first, first + count
        if first == 0:
            layer(0, lambda f, rows8: jnp.where(even_slab, end_b[f, rows8, :], end_a[f, rows8, :]), inside(0, 1))
            begin = 1
        elif first == nz // 2:
            layer(first, inside(first, -1), inside(first, 1))
            begin = first + 1
        if end in (nz // 2, nz):
            end -= 1
        lax.fori_loop(begin, end, lambda z, n: body(z, n), 0)
        if end == nz // 2 - 1:
            for pair in copies:
                for copy in pair:
                    copy.wait()
            layer(end, inside(end, -1), inside(end, 1))
        if end == nz - 1:
            layer(end, inside(end, -1), lambda f, rows8: jnp.where(even_slab, end_a[f, rows8, :], end_b[f, rows8, :]))
        sends.append(send(n, first, count))
        sends[-1].start()
    for copy in sends:
        copy.wait()


def stencil(mag, vel, kept, *halos):
    nz, nr, cells = mag.shape[1:]
    return pl.pallas_call(
        stencil_kernel,
        out_shape=(pltpu.HBM(mag.shape, F32), pltpu.VMEM((3, nz, 8, cells), F32)),
        in_specs=[HBM] * 2 + [VMEM] * 5,
        out_specs=(HBM, VMEM),
        scratch_shapes=[
            pltpu.VMEM(kept.shape, F32),
            pltpu.VMEM(mag.shape, F32),
            pltpu.VMEM((4, nr // 8, 8, cells), F32),
            pltpu.VMEM((6, 2, 8, cells), F32),
            pltpu.SemaphoreType.DMA((2, nz // 8)),
            pltpu.SemaphoreType.DMA((5,)),
        ],
        compiler_params=params(16),
        cost_estimate=cost(40 << 20, 8 << 20),
        name="stencil",
    )(*pinned(mag, vel), *resident(kept), *halos)


def decode_kernel(arrived, table, layers, edge, held, flux, out, fixed, sem):
    del held
    nz, cells = flux.shape[1:]
    high, low = split(jnp.transpose(arrived[...], (1, 0)))
    total = jnp.zeros((4 * nz, 2 * cells), F32)
    for i in range(4):
        part = slice(i * 2 * nz, (i + 1) * 2 * nz)
        pair = jnp.concatenate([high[part], low[part]], 0)
        total = total + dot(pair, table[i], NN)
    total = total[:, 0:cells] + total[:, cells : 2 * cells]
    total = (total[0 : 2 * nz] + total[2 * nz : 4 * nz]).reshape(2, nz, cells)
    thickness = layers[...].astype(F32) * (1.0 / LW)
    for c in range(2):
        fixed[c] = edge[c] - (thickness * total[c])[:, None, :] * edge[2]
    put = pltpu.make_async_copy(fixed, out.at[1:3, :, 56:64, :], sem)
    put.start()
    flux[...] = total
    put.wait()


def decode(arrived, table, layers, edge, held):
    nz, nr, cells = held.shape[1:]
    return pl.pallas_call(
        decode_kernel,
        out_shape=(
            jax.ShapeDtypeStruct((2, nz, cells), F32),
            pltpu.HBM(held.shape, F32),
        ),
        in_specs=[VMEM, VMEM, VMEM, VMEM, HBM],
        out_specs=(VMEM, HBM),
        scratch_shapes=[pltpu.VMEM((2, nz, 8, cells), F32), pltpu.SemaphoreType.DMA],
        input_output_aliases={4: 1},
        compiler_params=params(8),
        cost_estimate=cost(12 << 20, 1 << 20),
        name="decode",
    )(arrived, *resident(table), layers.reshape(1, cells), *resident(edge), *pinned(held))


def swap(payload, axis, offset, periodic):
    count = lax.axis_size(axis)
    pairs = []
    for i in range(offset, count - 1 + offset, 2):
        j = i + 1
        if j < count or periodic:
            pairs += [(i, j % count), (j % count, i)]
    return lax.ppermute(payload, axis, pairs)


def shards(magnetic, velocity, wall_response, mode_slots, wall_layers):
    message, table, ends_a, ends_b, near = encode(magnetic, velocity, mode_slots, wall_response)
    arrived = lax.all_to_all(message, BOTH, 0, 0, tiled=True)
    end_b = swap(ends_b, "slab", 1, False)
    end_a = swap(ends_a, "slab", 0, False)
    replies = apply_wall(arrived, near, wall_response)
    returned = lax.all_to_all(replies, BOTH, 0, 0, tiled=True)
    sides, kept = pack(magnetic, velocity, replies)
    side_b = swap(sides, "region", 1, True)
    side_a = swap(sides, "region", 0, True)
    stepped, edge = stencil(magnetic, velocity, kept, side_a, side_b, end_a, end_b)
    wall_flux, magnetic_next = decode(returned, table, wall_layers, edge, stepped)
    return magnetic_next, wall_flux


def solution(mesh):
    placed = (
        P(None, "slab", None, "region"),
        P(None, "slab", None, "region"),
        P(BOTH, None, None),
        P(),
        P("region"),
    )
    return jax.shard_map(
        shards,
        mesh=mesh,
        in_specs=placed,
        out_specs=(P(None, "slab", None, "region"), P(None, "slab", "region")),
        check_vma=False,
    )
```

```python
import math

import jax
import jax.numpy as jnp
from jax import lax
from jax.experimental import pallas as pl
from jax.experimental.pallas import tpu as pltpu
from jax.sharding import PartitionSpec as P

LW = 8
TIME_STEP = 0.0003
DIFFUSIVITY = 0.001
RADIAL_STEP = 1.0 / 384.0
AXIAL_STEP = 1.0 / 768.0

F32 = jnp.float32
BF16 = jnp.bfloat16
BOTH = ("region", "slab")
VMEM = pl.BlockSpec(memory_space=pltpu.VMEM)
ANY = pl.BlockSpec(memory_space=pl.ANY)
HBM = pl.BlockSpec(memory_space=pltpu.HBM)
NT = (((1,), (1,)), ((), ()))
NN = (((1,), (0,)), ((), ()))


def pinned(*arrays):
    return [pltpu.with_memory_space_constraint(a, pltpu.HBM) for a in arrays]


def resident(*arrays):
    return [pltpu.with_memory_space_constraint(a, pltpu.VMEM) for a in arrays]


def params(mib):
    return pltpu.CompilerParams(vmem_limit_bytes=mib * 1024 * 1024)


def cost(flops, nbytes):
    return pl.CostEstimate(flops=flops, bytes_accessed=nbytes, transcendentals=0)


def lanes(shape):
    return lax.broadcasted_iota(jnp.int32, shape, len(shape) - 1)


def rows(shape):
    return lax.broadcasted_iota(jnp.int32, shape, len(shape) - 2)


def split(x):
    high = x.astype(BF16)
    return high, (x - high.astype(F32)).astype(BF16)


def dot(a, b, dims):
    return lax.dot_general(a, b, dims, preferred_element_type=F32)


def half_turn_sine(phase, total):
    half = phase - total
    fold = jnp.abs(half)
    fold = jnp.minimum(fold, total - fold)
    x = fold.astype(F32) * (math.pi / total)
    y = x * x
    poly = -1.0 / math.factorial(11)
    for n, sign in ((9, 1.0), (7, -1.0), (5, 1.0), (3, -1.0)):
        poly = poly * y + sign / math.factorial(n)
    value = x + x * (y * poly)
    return jnp.where(half < 0, value, -value)


def block_transpose(x, width):
    r, b = rows(x.shape), lanes(x.shape) // width
    n, m = x.shape
    for bit in range(3):
        h = 1 << bit
        down = pltpu.roll(pltpu.roll(x, h, 0), m - width * h, 1)
        up = pltpu.roll(pltpu.roll(x, n - h, 0), width * h, 1)
        rb, bb = (r >> bit) & 1, (b >> bit) & 1
        x = jnp.where(rb == bb, x, jnp.where(rb == 1, down, up))
    return x


def encode_kernel(mag, vel, modes, wall, message, parts, ends_a, ends_b, near, rows_out, edge, slots, turned, sems, end_sems):
    count, cells = parts.shape[1], edge.shape[3]
    nmodes = 4 * count
    get_modes = pltpu.make_async_copy(modes, slots, sems.at[0])
    get_edge = pltpu.make_async_copy(mag.at[1:3, :, 56:64, :], edge, sems.at[1])
    get_modes.start()
    get_edge.start()
    odd = lax.axis_index("slab") % 2
    last = mag.shape[1] - 1
    ends = []
    for k, ref in enumerate((mag, vel)):
        for n, (target, layer) in enumerate(((ends_a, last * (1 - odd)), (ends_b, last * odd))):
            ends.append(
                pltpu.make_async_copy(ref.at[:, layer], target.at[pl.ds(3 * k, 3)], end_sems.at[k, n])
            )
            ends[-1].start()
    ends.append(pltpu.make_async_copy(wall.at[pl.ds(0, near.shape[0])], near, sems.at[2]))
    ends[-1].start()
    first = lax.axis_index("region") * cells
    odd_cell = (2 * (first + lanes((cells, cells))) + 1).astype(F32)
    get_modes.wait()
    filler = jnp.zeros((120, 128), F32)
    turned[...] = jnp.transpose(jnp.concatenate([slots[...].astype(F32), filler], 0), (1, 0))
    for i in range(4):
        strip = turned[pl.ds(i, 32, stride=4), :]
        for half in range(count // 128):
            columns = [strip[:, half * 4 + q : half * 4 + q + 1] for q in range(4)]
            mode = jnp.concatenate([jnp.broadcast_to(c, (32, cells)) for c in columns], 0)
            mode = mode.astype(jnp.int32)
            phase = (((mode + 1) >> 1).astype(F32) * odd_cell).astype(jnp.int32)
            phase = jnp.where((mode & 1) == 1, phase, phase + nmodes // 2) & (2 * nmodes - 1)
            high, low = split(half_turn_sine(phase, nmodes))
            part = slice(half * 128, half * 128 + 128)
            parts[i, part, 0:cells] = high
            parts[i, part, cells : 2 * cells] = low
    get_edge.wait()
    trace = edge[:, :, 7, :].reshape(32, cells)
    high, low = split(jnp.concatenate([trace] * 4, 0))
    weights = jnp.concatenate([jnp.concatenate([p, p], 1) for p in (high, low)], 0)
    lane = lanes((count, 128)) // 32
    out = jnp.zeros((count, 128), F32)
    for i in range(4):
        strip = turned[pl.ds(i, 32, stride=4), :]
        single = (strip == 0.0) | (strip == float(nmodes - 1))
        strip = jnp.where(single, 1.0 / nmodes, 2.0 / nmodes)
        scale = [jnp.broadcast_to(strip[:, r : r + 1], (32, 128)) for r in range(count // 32)]
        both = dot(parts[i], weights, NT)
        both = (both[:, 0:128] + both[:, 128:256]) * jnp.concatenate(scale, 0)
        out = jnp.where(lane == i, both, out)
    rows_out[...] = out
    ends.append(pltpu.make_async_copy(rows_out, message, sems.at[3]))
    ends[-1].start()
    for copy in ends:
        copy.wait()


def encode(mag, vel, modes, wall):
    nz, nr, cells = mag.shape[1:]
    count = modes.size // 4
    layer = pltpu.VMEM((6, nr, cells), F32)
    return pl.pallas_call(
        encode_kernel,
        out_shape=(
            pltpu.HBM((count, 128), F32),
            pltpu.VMEM((4, count, 2 * cells), BF16),
            layer,
            layer,
            pltpu.VMEM((2, *wall.shape[1:]), F32),
        ),
        in_specs=[HBM] * 4,
        out_specs=(HBM,) + (VMEM,) * 4,
        scratch_shapes=[
            pltpu.VMEM((count, 128), F32),
            pltpu.VMEM((2, nz, 8, cells), F32),
            pltpu.VMEM((8, 128), jnp.int32),
            pltpu.VMEM((128, 128), F32),
            pltpu.SemaphoreType.DMA((4,)),
            pltpu.SemaphoreType.DMA((2, 2)),
        ],
        compiler_params=params(8),
        cost_estimate=cost(3 * 2 * 1024 * 128 * 128, 1 << 20),
        name="encode",
    )(*pinned(mag, vel, modes.reshape(8, 128), wall))


def wall_kernel(arrived, near, wall, message, held, sems):
    count = near.shape[0]
    copies = [pltpu.make_async_copy(wall.at[count + i], held.at[i], sems.at[i]) for i in range(held.shape[0])]
    for copy in copies:
        copy.start()
    x = arrived[0:32, :]
    for r in range(1, 8):
        x = x + arrived[r * 32 : (r + 1) * 32, :]
    x = block_transpose(x, 16)
    coeff = jnp.concatenate([x[g * 8 : (g + 1) * 8] for g in range(4)], 1)
    stacked = jnp.concatenate([p.astype(F32) for p in split(coeff)], 0).astype(BF16)
    response = jnp.zeros(coeff.shape, F32)
    owner = rows(coeff.shape) >> 1
    for i in range(4):
        if i < count:
            high, low = split(near[i])
        else:
            copies[i - count].wait()
            high, low = split(held[i - count])
        a = dot(stacked, high, NT)
        b = dot(stacked, low, NT)
        response = jnp.where(owner == i, a[0:8] + (a[8:16] + b[0:8]), response)
    y = jnp.concatenate([response[:, g * 128 : (g + 1) * 128] for g in range(4)], 0)
    y = block_transpose(y, 16)
    for r in range(8):
        message[r * 32 : (r + 1) * 32, :] = y


def apply_wall(arrived, near, wall):
    return pl.pallas_call(
        wall_kernel,
        out_shape=jax.ShapeDtypeStruct(arrived.shape, F32),
        in_specs=[VMEM, VMEM, HBM],
        out_specs=VMEM,
        scratch_shapes=[
            pltpu.VMEM((wall.shape[0] - near.shape[0], *wall.shape[1:]), F32),
            pltpu.SemaphoreType.DMA((wall.shape[0] - near.shape[0],)),
        ],
        compiler_params=params(16),
        cost_estimate=cost(1 << 10, 1 << 10),
        name="wall",
    )(arrived, *resident(near), *pinned(wall))


def fetch(mag, vel, first, held, sems):
    return [
        [
            pltpu.make_async_copy(
                ref.at[:, pl.ds(first + part * 4, 4)], held.at[k, :, pl.ds(part * 4, 4)], sems.at[k, part]
            )
            for k, ref in enumerate((mag, vel))
        ]
        for part in range(held.shape[2] // 4)
    ]


def pack_kernel(mag, vel, earlier, sides, kept, held, kept_sems, held_sems):
    del earlier
    nz, nr, cells = mag.shape[1:]
    lane = lanes((8, cells))
    halves = ((kept, fetch(mag, vel, 0, kept, kept_sems)), (held, fetch(mag, vel, nz // 2, held, held_sems)))
    for _, copies in halves:
        for pair in copies:
            for copy in pair:
                copy.start()
    for half, (ref, copies) in enumerate(halves):
        out = [jnp.zeros((8, cells), F32)] * 6
        for z in range(nz // 2):
            if z % 4 == 0:
                for copy in copies[z // 4]:
                    copy.wait()
            for t in range(8):
                j = 2 * (z * 8 + t)
                here = (lane == j) | (lane == ((j + 127) & 127))
                for f in range(6):
                    tile = pltpu.roll(ref[f // 3, f % 3, z, t * 8 : (t + 1) * 8, :], j, 1)
                    out[f] = jnp.where(here, tile, out[f])
        for f in range(6):
            sides[f, half] = out[f]


def pack(mag, vel, earlier):
    nz, nr, cells = mag.shape[1:]
    return pl.pallas_call(
        pack_kernel,
        out_shape=(pltpu.VMEM((6, 2, 8, cells), F32), pltpu.VMEM((2, 3, nz // 2, nr, cells), F32)),
        in_specs=[HBM, HBM, ANY],
        out_specs=(VMEM, VMEM),
        scratch_shapes=[
            pltpu.VMEM((2, 3, nz // 2, nr, cells), F32),
            pltpu.SemaphoreType.DMA((2, nz // 8)),
            pltpu.SemaphoreType.DMA((2, nz // 8)),
        ],
        compiler_params=params(12),
        cost_estimate=cost(40 << 30, 8 << 30),
        name="pack",
    )(*pinned(mag, vel), earlier)


def stencil_kernel(mag, vel, kept, side_a, side_b, end_a, end_b, out, edge, held, stepped, factors, sides, gets, sems):
    nz, nr, cells = mag.shape[1:]
    lane = lanes((8, cells))
    row = rows((8, cells))
    copies = fetch(mag, vel, nz // 2, held, gets)
    for pair in copies:
        for copy in pair:
            copy.start()
    even = lax.axis_index("region") % 2 == 0
    for f in range(6):
        for half in range(2):
            a, b = side_a[f, half], side_b[f, half]
            low = pltpu.roll(jnp.where(even, b, a), 1, 1)
            high = pltpu.roll(jnp.where(even, a, b), cells - 1, 1)
            sides[f, half] = jnp.where(lane % 2 == 0, low, high)
    even_slab = lax.axis_index("slab") % 2 == 0
    angle_step = 2.0 * math.pi / (cells * 8)
    spread = TIME_STEP * DIFFUSIVITY
    by_radial = TIME_STEP / (2.0 * RADIAL_STEP)
    by_axial = TIME_STEP / (2.0 * AXIAL_STEP)
    second_radial = spread / RADIAL_STEP**2
    second_axial = spread / AXIAL_STEP**2
    for t in range(nr // 8):
        radius = 1.0 - (nr - (t * 8 + row).astype(F32) - 0.5) * RADIAL_STEP
        arc = 1.0 / (radius * angle_step)
        second = spread * arc * arc
        factors[0, t] = (0.5 * TIME_STEP) * arc
        factors[1, t] = (spread / (2.0 * RADIAL_STEP)) / radius
        factors[2, t] = second
        factors[3, t] = 1.0 - 2.0 * (second + (second_radial + second_axial))

    def layer(z, down, up):
        field, place = whose(z)
        for t in range(nr // 8):
            j = (z & 7) * 8 + t
            rows8 = slice(t * 8, t * 8 + 8)
            x, dr, dp, dz, sr, sp, sz = [], [], [], [], [], [], []
            for f in range(6):
                ref, c = field.at[f // 3, f % 3], place
                here = ref[c, rows8, :]
                if t == 0:
                    inner = jnp.where(row == 0, here, pltpu.roll(here, 1, 0))
                else:
                    inner = ref[c, t * 8 - 1 : t * 8 + 7, :]
                if t == nr // 8 - 1:
                    outer = jnp.where(row == 7, here, pltpu.roll(here, 7, 0))
                else:
                    outer = ref[c, t * 8 + 1 : t * 8 + 9, :]
                beyond = pltpu.roll(sides[f, z >> 3], (256 - 2 * j) & 127, 1)
                p_next = jnp.where(lane == cells - 1, beyond, pltpu.roll(here, cells - 1, 1))
                p_prev = jnp.where(lane == 0, beyond, pltpu.roll(here, 1, 1))
                z_next = up(f, rows8)
                z_prev = down(f, rows8)
                x.append(here)
                dr.append(outer - inner)
                dp.append(p_next - p_prev)
                dz.append(z_next - z_prev)
                if f < 3:
                    sr.append(outer + inner)
                    sp.append(p_next + p_prev)
                    sz.append(z_next + z_prev)
            turn, curve, second, keep = (factors[n, t] for n in range(4))
            ur = curve - by_radial * x[3]
            up_ = turn * x[4]
            uz = by_axial * x[5]
            br = by_radial * x[0]
            bp = turn * x[1]
            bz = by_axial * x[2]
            for c in range(3):
                value = keep * x[c] + second_radial * sr[c] + (second * sp[c] + second_axial * sz[c])
                value = value + (ur * dr[c] - up_ * dp[c]) - uz * dz[c]
                value = value + (br * dr[c + 3] + bp * dp[c + 3]) + bz * dz[c + 3]
                stepped[c, z, rows8, :] = value
                if c and t == nr // 8 - 1:
                    edge[c - 1, z] = value
            if t == nr // 8 - 1:
                at_wall = second_radial + spread / (2.0 * RADIAL_STEP) / (1.0 - 0.5 * RADIAL_STEP)
                edge[2, z] = jnp.where(row == 7, at_wall - by_radial * x[3], 0.0)

    def inside(z, step):
        field, place = whose(z, step)
        return lambda f, rows8: field[f // 3, f % 3, place, rows8, :]

    def send(n, first, count):
        part = pl.ds(first, count)
        return pltpu.make_async_copy(stepped.at[:, part], out.at[:, part], sems.at[n])

    def whose(z, step=0):
        if isinstance(z, int):
            return (kept, z + step) if z + step < nz // 2 else (held, z + step - nz // 2)
        return (kept, z + step) if in_kept[0] else (held, z + step - nz // 2)

    def body(z, _):
        layer(z, inside(z, -1), inside(z, 1))
        return 0

    in_kept = [True]
    sends = []
    for n, (first, count) in enumerate(((0, 4), (4, 4), (8, 4), (12, 2), (14, 2))):
        if first == nz // 2:
            in_kept[0] = False
        begin, end = first, first + count
        if first == 0:
            layer(0, lambda f, rows8: jnp.where(even_slab, end_b[f, rows8, :], end_a[f, rows8, :]), inside(0, 1))
            begin = 1
        elif first == nz // 2:
            layer(first, inside(first, -1), inside(first, 1))
            begin = first + 1
        if end in (nz // 2, nz):
            end -= 1
        lax.fori_loop(begin, end, lambda z, n: body(z, n), 0)
        if end == nz // 2 - 1:
            for pair in copies:
                for copy in pair:
                    copy.wait()
            layer(end, inside(end, -1), inside(end, 1))
        if end == nz - 1:
            layer(end, inside(end, -1), lambda f, rows8: jnp.where(even_slab, end_a[f, rows8, :], end_b[f, rows8, :]))
        sends.append(send(n, first, count))
        sends[-1].start()
    for copy in sends:
        copy.wait()


def stencil(mag, vel, kept, *halos):
    nz, nr, cells = mag.shape[1:]
    return pl.pallas_call(
        stencil_kernel,
        out_shape=(pltpu.HBM(mag.shape, F32), pltpu.VMEM((3, nz, 8, cells), F32)),
        in_specs=[HBM] * 2 + [VMEM] * 5,
        out_specs=(HBM, VMEM),
        scratch_shapes=[
            pltpu.VMEM(kept.shape, F32),
            pltpu.VMEM(mag.shape, F32),
            pltpu.VMEM((4, nr // 8, 8, cells), F32),
            pltpu.VMEM((6, 2, 8, cells), F32),
            pltpu.SemaphoreType.DMA((2, nz // 8)),
            pltpu.SemaphoreType.DMA((5,)),
        ],
        compiler_params=params(16),
        cost_estimate=cost(40 << 20, 8 << 20),
        name="stencil",
    )(*pinned(mag, vel), *resident(kept), *halos)


def decode_kernel(arrived, table, layers, edge, held, flux, out, fixed, total_out, sems):
    del held
    nz, cells = flux.shape[1:]
    high, low = split(jnp.transpose(arrived[...], (1, 0)))
    total = jnp.zeros((4 * nz, 2 * cells), F32)
    for i in range(4):
        part = slice(i * 2 * nz, (i + 1) * 2 * nz)
        pair = jnp.concatenate([high[part], low[part]], 0)
        total = total + dot(pair, table[i], NN)
    total = total[:, 0:cells] + total[:, cells : 2 * cells]
    total = (total[0 : 2 * nz] + total[2 * nz : 4 * nz]).reshape(2, nz, cells)
    total_out[...] = total
    put_flux = pltpu.make_async_copy(total_out, flux, sems.at[0])
    put_flux.start()
    thickness = layers[...].astype(F32) * (1.0 / LW)
    for c in range(2):
        fixed[c] = edge[c] - (thickness * total[c])[:, None, :] * edge[2]
    put = pltpu.make_async_copy(fixed, out.at[1:3, :, 56:64, :], sems.at[1])
    put.start()
    put_flux.wait()
    put.wait()


def decode(arrived, table, layers, edge, held):
    nz, nr, cells = held.shape[1:]
    return pl.pallas_call(
        decode_kernel,
        out_shape=(
            pltpu.HBM((2, nz, cells), F32),
            pltpu.HBM(held.shape, F32),
        ),
        in_specs=[VMEM, VMEM, VMEM, VMEM, HBM],
        out_specs=(HBM, HBM),
        scratch_shapes=[
            pltpu.VMEM((2, nz, 8, cells), F32),
            pltpu.VMEM((2, nz, cells), F32),
            pltpu.SemaphoreType.DMA((2,)),
        ],
        input_output_aliases={4: 1},
        compiler_params=params(8),
        cost_estimate=cost(12 << 20, 1 << 20),
        name="decode",
    )(arrived, *resident(table), layers.reshape(1, cells), *resident(edge), *pinned(held))


def swap(payload, axis, offset, periodic):
    count = lax.axis_size(axis)
    pairs = []
    for i in range(offset, count - 1 + offset, 2):
        j = i + 1
        if j < count or periodic:
            pairs += [(i, j % count), (j % count, i)]
    return lax.ppermute(payload, axis, pairs)


def shards(magnetic, velocity, wall_response, mode_slots, wall_layers):
    message, table, ends_a, ends_b, near = encode(magnetic, velocity, mode_slots, wall_response)
    arrived = lax.all_to_all(message, BOTH, 0, 0, tiled=True)
    end_b = swap(ends_b, "slab", 1, False)
    end_a = swap(ends_a, "slab", 0, False)
    replies = apply_wall(arrived, near, wall_response)
    returned = lax.all_to_all(replies, BOTH, 0, 0, tiled=True)
    sides, kept = pack(magnetic, velocity, replies)
    side_b = swap(sides, "region", 1, True)
    side_a = swap(sides, "region", 0, True)
    stepped, edge = stencil(magnetic, velocity, kept, side_a, side_b, end_a, end_b)
    wall_flux, magnetic_next = decode(returned, table, wall_layers, edge, stepped)
    return magnetic_next, wall_flux


def solution(mesh):
    placed = (
        P(None, "slab", None, "region"),
        P(None, "slab", None, "region"),
        P(BOTH, None, None),
        P(),
        P("region"),
    )
    return jax.shard_map(
        shards,
        mesh=mesh,
        in_specs=placed,
        out_specs=(P(None, "slab", None, "region"), P(None, "slab", "region")),
        check_vma=False,
    )
```
